256 devices in a mesh: sample: 2 (over z_lo), seq: 128 (over x, y, z_hi, core).
Axes of the slice: x: 4, y: 4, z: 8 (z_hi: 4, z_lo: 2; z = z_hi * 2 + z_lo), core: 2. Of those that a mesh axis runs over, the one named last changes fastest.
Arguments:
- grad_out: bfloat16 [4, 64, 128, 1152], P('sample', None, 'seq'), may hold values from -6 to 6
- t_query: bfloat16 [4, 64, 128, 1152], P('sample', None, 'seq'), may hold values from -200 to 200
- t_key: bfloat16 [4, 64, 128, 1152], P('sample', None, 'seq'), may hold values from -4 to 4
- t_value: bfloat16 [4, 64, 128, 1152], P('sample', None, 'seq'), may hold values from -6 to 6
- t_out_weight: bfloat16 [1152, 1152], P('seq'), may hold values from -0.1875 to 0.1875
- t_qkv_weight: bfloat16 [1152, 3456], P('seq'), may hold values from -0.1875 to 0.1875
- frame_input: bfloat16 [256, 128, 1152], P(('sample', 'seq')), may hold values from -6 to 6
- cross_weights: bfloat16 [2, 1152, 1152], P(None, 'sample'), may hold values from -0.1875 to 0.1875
- cap_key: bfloat16 [300, 1152], replicated, may hold values from -160 to 160
- cap_value: bfloat16 [300, 1152], replicated, may hold values from -6 to 6
- cap_length: int32 [1], replicated, may hold values from 75 to 300
Outputs:
- grad_input: bfloat16 [256, 128, 1152], P(('sample', 'seq'))
- caption_grad: float32 [300, 2304], P(None, ('sample', 'seq'))
The draws below stay inside these ranges and needn't reach their ends.
All inputs are finite; a program needn't handle non-finite values.
Results may differ from the reference program's by a relative error of at most 0.028.
The reference program's roundings to bfloat16 on the way count: a program that leaves them out, or rounds other values in their place, can miss the bound.
Values may be sent and summed in bfloat16 or wider, within the bound.
No kernel may reach another device: no remote copies, remote signals or barrier semaphores. Data moves between devices by JAX's collectives and lax.ppermute only.
A program may use at most 128 MiB of HBM per device.

```python
import math
import jax
import jax.numpy as jnp
from jax import lax

D = 1152
HEADS = 16
HEAD_DIM = 72
CAP = 300
FRAMES = 64
SAMPLES = 4
PATCHES = 128


def shared_keys(key):
    return jnp.clip(jax.random.normal(key, (SAMPLES, FRAMES, PATCHES, D), jnp.float32), -4.0, 4.0)


def draw_t_key(key, part):
    common = shared_keys(key)
    return common.astype(jnp.bfloat16)


def draw_t_query(key, part):
    key = jax.random.fold_in(key, 5)
    shape = (SAMPLES, FRAMES, PATCHES, D)
    values = jnp.clip(jax.random.normal(key, shape, jnp.float32), -4.0, 4.0)
    return values.astype(jnp.bfloat16)


def draw_cap_key(key, part):
    key = jax.random.fold_in(key, 7)
    values = jnp.clip(jax.random.normal(key, (CAP, D), jnp.float32), -4.0, 4.0)
    return values.astype(jnp.bfloat16)


def steps_of(rng, shape, shards, low, largest):
    factor_of = 1.0
    for dim, blocks in shards:
        draws = jax.random.uniform(jax.random.fold_in(jax.random.fold_in(rng, 6), dim), (blocks,), jnp.float32, low / len(shards), largest / len(shards))
        factor_of = factor_of * jnp.repeat(jnp.exp(draws), shape[dim] // blocks).reshape((-1,) + (1,) * (len(shape) - 1 - dim))
    return factor_of


def scatter_about(rng, extent, deviation, reach, shards=(), held_as=jnp.bfloat16):
    loudness = steps_of(rng, extent, shards, -0.22, 0.18) if shards else 1.0
    values = jax.random.normal(rng, extent, jnp.float32) * deviation * loudness
    return jnp.minimum(jnp.maximum(values, -reach), reach).astype(held_as)


def setup_inputs(seed: int = 0) -> dict:
    splits = jax.random.split(jax.random.key(seed), 12)
    return {
        "grad_out": scatter_about(splits[0], (SAMPLES, FRAMES, PATCHES, D), 1.0, 6.0, ((0, 2), (2, 128))),
        "t_query": draw_t_query(jax.random.fold_in(splits[11], 71), 0),
        "t_key": draw_t_key(jax.random.fold_in(splits[11], 71), 0),
        "t_value": scatter_about(splits[3], (SAMPLES, FRAMES, PATCHES, D), 1.0, 6.0, ((0, 2), (2, 128))),
        "t_out_weight": scatter_about(splits[4], (D, D), D ** -0.5, 0.1875, ((0, 128),)),
        "t_qkv_weight": scatter_about(splits[5], (D, 3 * D), D ** -0.5, 0.1875, ((0, 128),)),
        "frame_input": scatter_about(splits[6], (SAMPLES * FRAMES, PATCHES, D), 1.0, 6.0, ((0, 256),)),
        "cross_weights": scatter_about(splits[7], (2, D, D), D ** -0.5, 0.1875, ((1, 2),)),
        "cap_key": draw_cap_key(jax.random.fold_in(splits[11], 71), 0),
        "cap_value": scatter_about(splits[9], (CAP, D), 1.0, 6.0),
        "cap_length": jax.random.randint(splits[10], (1,), CAP // 4, CAP + 1).astype(jnp.int32),
    }


def split_heads(tensor):
    return tensor.reshape(tensor.shape[:-1] + (HEADS, HEAD_DIM))

def widen(tensor):
    return lax.optimization_barrier(tensor).astype(jnp.float32)

def temporal_sample(arrays, t_out_weight, t_qkv_weight):
    grad_block, query, key_rows, value = arrays
    scaling = 1.0 / math.sqrt(HEAD_DIM)
    grad_rows = grad_block.reshape(-1, D)
    grad_heads = jnp.dot(grad_rows, t_out_weight.T, preferred_element_type=jnp.float32).astype(jnp.bfloat16)
    grad_split = split_heads(widen(grad_heads).reshape(grad_block.shape))
    query_split = split_heads(query.astype(jnp.float32))
    key_split = split_heads(key_rows.astype(jnp.float32))
    value_split = split_heads(value.astype(jnp.float32))
    scores = jnp.einsum('fphd,gphd->phfg', query_split, key_split) * scaling
    attention = jax.nn.softmax(scores, axis=-1)
    attention_low = widen(attention.astype(jnp.bfloat16))
    value_grad = jnp.einsum('phfg,fphd->gphd', attention_low, grad_split).astype(jnp.bfloat16)
    prob_grad = jnp.einsum('fphd,gphd->phfg', grad_split, value_split)
    centred = prob_grad - lax.optimization_barrier(jnp.sum(prob_grad * attention, axis=-1, keepdims=True))
    score_grad = widen((attention * centred * scaling).astype(jnp.bfloat16))
    query_grad = jnp.einsum('phfg,gphd->fphd', score_grad, key_split).astype(jnp.bfloat16)
    key_grad = jnp.einsum('phfg,fphd->gphd', score_grad, query_split).astype(jnp.bfloat16)
    joined = jnp.concatenate([query_grad.reshape(-1, D), key_grad.reshape(-1, D), value_grad.reshape(-1, D)], axis=-1)
    mixed = grad_rows.astype(jnp.float32) + jnp.dot(joined, t_qkv_weight.T, preferred_element_type=jnp.float32)
    return mixed.astype(jnp.bfloat16).reshape(grad_block.shape)

def cross_slot(x_rows, d_rows, w_query, w_out, cap_key, cap_value, valid_keys):
    scaling = 1.0 / math.sqrt(HEAD_DIM)
    cross_query = jnp.dot(x_rows, w_query, preferred_element_type=jnp.float32).astype(jnp.bfloat16)
    out_grad = jnp.dot(d_rows, w_out.T, preferred_element_type=jnp.float32).astype(jnp.bfloat16)
    query_split = split_heads(widen(cross_query))
    output_split = split_heads(widen(out_grad))
    key_split = split_heads(cap_key.astype(jnp.float32))
    value_split = split_heads(cap_value.astype(jnp.float32))
    scores = jnp.einsum('nhd,chd->nhc', query_split, key_split) * scaling
    scores = jnp.where(valid_keys[None, None, :], scores, -1e+30)
    attention = jax.nn.softmax(scores, axis=-1)
    attention_low = widen(attention.astype(jnp.bfloat16))
    prob_grad = jnp.einsum('nhd,chd->nhc', output_split, value_split)
    centred = prob_grad - lax.optimization_barrier(jnp.sum(prob_grad * attention, axis=-1, keepdims=True))
    score_grad = widen((attention * centred * scaling).astype(jnp.bfloat16))
    cq_grad = jnp.einsum('nhc,chd->nhd', score_grad, key_split).astype(jnp.bfloat16).reshape(-1, D)
    result = (d_rows.astype(jnp.float32) + jnp.dot(cq_grad, w_query.T, preferred_element_type=jnp.float32)).astype(jnp.bfloat16)
    key_term = jnp.einsum('nhc,nhd->chd', score_grad, query_split).reshape(-1, D)
    value_term = jnp.einsum('nhc,nhd->chd', attention_low, output_split).reshape(-1, D)
    return (result, jnp.concatenate([key_term, value_term], axis=-1))

def reference(grad_out, t_query, t_key, t_value, t_out_weight, t_qkv_weight, frame_input, cross_weights, cap_key, cap_value, cap_length):
    mixed = lax.map(lambda arrays: temporal_sample(arrays, t_out_weight, t_qkv_weight), (grad_out, t_query, t_key, t_value))
    frame_rows = mixed.reshape(SAMPLES * FRAMES, PATCHES, D)
    valid_keys = jnp.arange(CAP) < cap_length[0]

    def advance(running, blocks):
        x_rows, d_rows = blocks
        result, term = cross_slot(x_rows, d_rows, cross_weights[0], cross_weights[1], cap_key, cap_value, valid_keys)
        return (running + term, result)
    running, results = lax.scan(advance, jnp.zeros((CAP, 2 * D), jnp.float32), (frame_input, frame_rows))
    return (results, running)
```

```python
import math

import jax
import jax.numpy as jnp
from jax import lax
from jax.sharding import Mesh, PartitionSpec as P

HEADS = 16
HEAD_DIM = 72


CONTRACT_LAST = (((1,), (1,)), ((), ()))


def split_heads(tensor):
    return tensor.reshape(tensor.shape[:-1] + (HEADS, HEAD_DIM))


def merge_heads(tensor):
    return tensor.reshape(tensor.shape[:-2] + (tensor.shape[-2] * tensor.shape[-1],))


def temporal_grads(grad_heads, query, key_rows, value):
    scaling = 1.0 / math.sqrt(HEAD_DIM)
    grad_split = split_heads(grad_heads)
    query_split = split_heads(query)
    key_split = split_heads(key_rows)
    value_split = split_heads(value)
    scores = (
        jnp.einsum("sfphd,sgphd->sphfg", query_split, key_split, preferred_element_type=jnp.float32)
        * scaling
    )
    attention = jax.nn.softmax(scores, axis=-1)
    attention_low = attention.astype(jnp.bfloat16)
    value_grad = jnp.einsum(
        "sphfg,sfphd->sgphd", attention_low, grad_split, preferred_element_type=jnp.float32
    ).astype(jnp.bfloat16)
    prob_grad = jnp.einsum(
        "sfphd,sgphd->sphfg", grad_split, value_split, preferred_element_type=jnp.float32
    )
    centred = prob_grad - jnp.sum(prob_grad * attention, axis=-1, keepdims=True)
    score_grad = (attention * centred * scaling).astype(jnp.bfloat16)
    query_grad = jnp.einsum(
        "sphfg,sgphd->sfphd", score_grad, key_split, preferred_element_type=jnp.float32
    ).astype(jnp.bfloat16)
    key_grad = jnp.einsum(
        "sphfg,sfphd->sgphd", score_grad, query_split, preferred_element_type=jnp.float32
    ).astype(jnp.bfloat16)
    return jnp.concatenate(
        [merge_heads(query_grad), merge_heads(key_grad), merge_heads(value_grad)], axis=-1
    )


def cross_grads(x_rows, d_rows, w_query, w_out, cap_key, cap_value, valid_keys):
    scaling = 1.0 / math.sqrt(HEAD_DIM)
    cross_query = jnp.dot(x_rows, w_query, preferred_element_type=jnp.float32).astype(jnp.bfloat16)
    out_grad = lax.dot_general(
        d_rows, w_out, CONTRACT_LAST, preferred_element_type=jnp.float32
    ).astype(jnp.bfloat16)
    query_split = split_heads(cross_query)
    output_split = split_heads(out_grad)
    key_split = split_heads(cap_key)
    value_split = split_heads(cap_value)
    scores = (
        jnp.einsum("nhd,chd->nhc", query_split, key_split, preferred_element_type=jnp.float32)
        * scaling
    )
    scores = jnp.where(valid_keys[None, None, :], scores, -1e30)
    attention = jax.nn.softmax(scores, axis=-1)
    attention_low = attention.astype(jnp.bfloat16)
    prob_grad = jnp.einsum(
        "nhd,chd->nhc", output_split, value_split, preferred_element_type=jnp.float32
    )
    centred = prob_grad - jnp.sum(prob_grad * attention, axis=-1, keepdims=True)
    score_grad = (attention * centred * scaling).astype(jnp.bfloat16)
    cq_grad = merge_heads(
        jnp.einsum(
            "nhc,chd->nhd", score_grad, key_split, preferred_element_type=jnp.float32
        ).astype(jnp.bfloat16)
    )
    result = (
        d_rows.astype(jnp.float32)
        + lax.dot_general(cq_grad, w_query, CONTRACT_LAST, preferred_element_type=jnp.float32)
    ).astype(jnp.bfloat16)
    key_term = jnp.einsum(
        "nhc,nhd->hdc", score_grad, query_split, preferred_element_type=jnp.float32
    )
    value_term = jnp.einsum(
        "nhc,nhd->hdc", attention_low, output_split, preferred_element_type=jnp.float32
    )
    return (result, jnp.concatenate([key_term, value_term], axis=1).astype(jnp.bfloat16))


ALL = ("s", "x", "y", "z", "c")
SEQ = ("x", "y", "z", "c")
SHAPE = (2, 4, 4, 4, 2)


def flat(s, x, y, z, c):
    return (((s * 4 + x) * 4 + y) * 4 + z) * 2 + c


def ring_groups(first):
    groups = []
    for s in range(2):
        for z in range(4):
            for fixed in range(4):
                groups.append([flat(s, i, fixed, z, first) for i in range(4)])
                groups.append([flat(s, fixed, i, z, 1 - first) for i in range(4)])
    return groups


def gather_groups(block, groups):
    copies = jnp.broadcast_to(block[None], (4,) + block.shape)
    return lax.all_to_all(copies, ALL, 0, 0, axis_index_groups=groups)


def gather_rows(block):
    core = lax.axis_index("c")
    near = gather_groups(block, ring_groups(0))
    whole = gather_groups(near, ring_groups(1))
    return whole


def both_cores(mine):
    core = lax.axis_index("c")
    other = lax.ppermute(mine, "c", [(0, 1), (1, 0)])
    rows = mine.shape[2] * 16
    first = jnp.where(core == 0, mine, other).transpose(1, 0, 2, 3)
    second = jnp.where(core == 0, other, mine)
    return first.reshape(rows, -1), second.reshape(rows, -1)


def cross_halves(cross_weights):
    core = lax.axis_index("c")
    side = lax.axis_index("s")

    def place(z):
        return (z % 2, z // 2)

    pairs = []
    for x in range(4):
        for y in range(4):
            for z in range(8):
                for c in range(2):
                    to = (z + (1 if c == 0 else 7)) % 8
                    s0, z0 = place(z)
                    s1, z1 = place(to)
                    pairs.append((flat(s0, x, y, z0, c), flat(s1, x, y, z1, c)))
    part = lax.dynamic_index_in_dim(cross_weights, core, 0, keepdims=False)
    got = lax.ppermute(part, ALL, pairs)
    swapped = lax.ppermute(got, "c", [(0, 1), (1, 0)])
    other = jnp.stack([jnp.where(core == 0, got, swapped), jnp.where(core == 0, swapped, got)])
    low = jnp.where(side == 0, cross_weights, other)
    high = jnp.where(side == 0, other, cross_weights)
    return jnp.concatenate([low, high], axis=1)


def local(
    grad_out,
    t_query,
    t_key,
    t_value,
    t_out_weight,
    t_qkv_weight,
    frame_input,
    cross_weights,
    cap_key,
    cap_value,
    cap_length,
):
    samp_here, frames, patch_here, width = grad_out.shape
    slot_shape = (samp_here * frames, patch_here, width)
    core = lax.axis_index("c")
    full_cross = cross_halves(cross_weights)
    grad_rows = grad_out.reshape(-1, width)
    shard = jnp.concatenate([t_out_weight, t_qkv_weight], axis=1).reshape(2, -1)
    column = lax.all_to_all(
        jnp.broadcast_to(shard[None], (8,) + shard.shape), ("z", "c"), 0, 0
    ).reshape(72, 4 * width)
    out_part = lax.dynamic_slice(column, (0, core * 512), (72, 640))
    qkv_part = lax.dynamic_slice(column, (0, 1152 + core * 1664), (72, 1792))
    out_first, out_second = both_cores(gather_rows(out_part))
    qkv_first, qkv_second = both_cores(gather_rows(qkv_part))
    grad_heads = (
        lax.dot_general(
            grad_rows[:, :640], out_first, CONTRACT_LAST, preferred_element_type=jnp.float32
        )
        + lax.dot_general(
            grad_rows[:, 640:],
            out_second[:, 128:],
            CONTRACT_LAST,
            preferred_element_type=jnp.float32,
        )
    ).astype(jnp.bfloat16)
    qkv_grad = temporal_grads(grad_heads.reshape(grad_out.shape), t_query, t_key, t_value).reshape(
        -1, 3 * width
    )
    product = lax.dot_general(
        qkv_grad[:, :1792], qkv_first, CONTRACT_LAST, preferred_element_type=jnp.float32
    ) + lax.dot_general(
        qkv_grad[:, 1792:],
        qkv_second[:, 128:],
        CONTRACT_LAST,
        preferred_element_type=jnp.float32,
    )
    mixed_rows = (grad_rows.astype(jnp.float32) + product).astype(jnp.bfloat16)
    valid_keys = jnp.arange(cap_key.shape[0]) < cap_length[0]
    arrived = lax.all_to_all(
        mixed_rows.reshape(slot_shape), SEQ, split_axis=0, concat_axis=1, tiled=True
    )
    result_rows, terms = cross_grads(
        frame_input.reshape(-1, width),
        arrived.reshape(-1, width),
        full_cross[0],
        full_cross[1],
        cap_key,
        cap_value,
        valid_keys,
    )
    grad_input = result_rows.reshape(frame_input.shape)
    head = jnp.sum(lax.all_to_all(terms, ("x", "y"), 0, 0).astype(jnp.float32), axis=0)
    pieces = head.astype(jnp.bfloat16).reshape(16, 9, -1)
    piece = jnp.sum(lax.all_to_all(pieces, ("s", "z", "c"), 0, 0).astype(jnp.float32), axis=0)
    return (grad_input, piece.T)


def solution(mesh):
    fine = Mesh(mesh.devices.reshape(SHAPE), ALL)
    return jax.shard_map(
        local,
        mesh=fine,
        in_specs=(
            P("s", None, SEQ, None),
            P("s", None, SEQ, None),
            P("s", None, SEQ, None),
            P("s", None, SEQ, None),
            P(SEQ, None),
            P(SEQ, None),
            P(ALL, None, None),
            P(None, "s", None),
            P(),
            P(),
            P(),
        ),
        out_specs=(P(ALL, None, None), P(None, ALL)),
        check_vma=False,
    )
```

```python
import math

import jax
import jax.numpy as jnp
from jax import lax
from jax.sharding import Mesh, PartitionSpec as P

HEADS = 16
HEAD_DIM = 72


CONTRACT_LAST = (((1,), (1,)), ((), ()))


def split_heads(tensor):
    return tensor.reshape(tensor.shape[:-1] + (HEADS, HEAD_DIM))


def merge_heads(tensor):
    return tensor.reshape(tensor.shape[:-2] + (tensor.shape[-2] * tensor.shape[-1],))


def temporal_grads(grad_heads, query, key_rows, value):
    scaling = 1.0 / math.sqrt(HEAD_DIM)
    grad_split = split_heads(grad_heads)
    query_split = split_heads(query)
    key_split = split_heads(key_rows)
    value_split = split_heads(value)
    scores = (
        jnp.einsum("sfphd,sgphd->sphfg", query_split, key_split, preferred_element_type=jnp.float32)
        * scaling
    )
    attention = jax.nn.softmax(scores, axis=-1)
    attention_low = attention.astype(jnp.bfloat16)
    value_grad = jnp.einsum(
        "sphfg,sfphd->sgphd", attention_low, grad_split, preferred_element_type=jnp.float32
    ).astype(jnp.bfloat16)
    prob_grad = jnp.einsum(
        "sfphd,sgphd->sphfg", grad_split, value_split, preferred_element_type=jnp.float32
    )
    centred = prob_grad - jnp.sum(prob_grad * attention, axis=-1, keepdims=True)
    score_grad = (attention * centred * scaling).astype(jnp.bfloat16)
    query_grad = jnp.einsum(
        "sphfg,sgphd->sfphd", score_grad, key_split, preferred_element_type=jnp.float32
    ).astype(jnp.bfloat16)
    key_grad = jnp.einsum(
        "sphfg,sfphd->sgphd", score_grad, query_split, preferred_element_type=jnp.float32
    ).astype(jnp.bfloat16)
    return jnp.concatenate(
        [merge_heads(query_grad), merge_heads(key_grad), merge_heads(value_grad)], axis=-1
    )


def cross_grads(x_rows, d_rows, w_query, w_out, cap_key, cap_value, valid_keys):
    scaling = 1.0 / math.sqrt(HEAD_DIM)
    cross_query = jnp.dot(x_rows, w_query, preferred_element_type=jnp.float32).astype(jnp.bfloat16)
    out_grad = lax.dot_general(
        d_rows, w_out, CONTRACT_LAST, preferred_element_type=jnp.float32
    ).astype(jnp.bfloat16)
    query_split = split_heads(cross_query)
    output_split = split_heads(out_grad)
    key_split = split_heads(cap_key)
    value_split = split_heads(cap_value)
    scores = (
        jnp.einsum("nhd,chd->nhc", query_split, key_split, preferred_element_type=jnp.float32)
        * scaling
    )
    scores = jnp.where(valid_keys[None, None, :], scores, -1e30)
    attention = jax.nn.softmax(scores, axis=-1)
    attention_low = attention.astype(jnp.bfloat16)
    prob_grad = jnp.einsum(
        "nhd,chd->nhc", output_split, value_split, preferred_element_type=jnp.float32
    )
    centred = prob_grad - jnp.sum(prob_grad * attention, axis=-1, keepdims=True)
    score_grad = (attention * centred * scaling).astype(jnp.bfloat16)
    cq_grad = merge_heads(
        jnp.einsum(
            "nhc,chd->nhd", score_grad, key_split, preferred_element_type=jnp.float32
        ).astype(jnp.bfloat16)
    )
    result = (
        d_rows.astype(jnp.float32)
        + lax.dot_general(cq_grad, w_query, CONTRACT_LAST, preferred_element_type=jnp.float32)
    ).astype(jnp.bfloat16)
    key_term = jnp.einsum(
        "nhc,nhd->hdc", score_grad, query_split, preferred_element_type=jnp.float32
    )
    value_term = jnp.einsum(
        "nhc,nhd->hdc", attention_low, output_split, preferred_element_type=jnp.float32
    )
    return (result, jnp.stack([key_term, value_term]).astype(jnp.bfloat16))


ALL = ("s", "x", "y", "z", "c")
SEQ = ("x", "y", "z", "c")
SHAPE = (2, 4, 4, 4, 2)


def flat(s, x, y, z, c):
    return (((s * 4 + x) * 4 + y) * 4 + z) * 2 + c


def ring_groups(first):
    groups = []
    for s in range(2):
        for z in range(4):
            for fixed in range(4):
                groups.append([flat(s, i, fixed, z, first) for i in range(4)])
                groups.append([flat(s, fixed, i, z, 1 - first) for i in range(4)])
    return groups


def gather_groups(block, groups):
    copies = jnp.broadcast_to(block[None], (4,) + block.shape)
    return lax.all_to_all(copies, ALL, 0, 0, axis_index_groups=groups)


def both_cores(mine):
    core = lax.axis_index("c")
    other = lax.ppermute(mine, "c", [(0, 1), (1, 0)])
    rows = mine.shape[2] * 16
    first = jnp.where(core == 0, mine, other).transpose(1, 0, 2, 3)
    second = jnp.where(core == 0, other, mine)
    return first.reshape(rows, -1), second.reshape(rows, -1)


def cross_halves(cross_weights):
    core = lax.axis_index("c")
    side = lax.axis_index("s")

    def place(z):
        return (z % 2, z // 2)

    pairs = []
    for x in range(4):
        for y in range(4):
            for z in range(8):
                for c in range(2):
                    to = (z + (1 if c == 0 else 7)) % 8
                    s0, z0 = place(z)
                    s1, z1 = place(to)
                    pairs.append((flat(s0, x, y, z0, c), flat(s1, x, y, z1, c)))
    part = lax.dynamic_index_in_dim(cross_weights, core, 0, keepdims=False)
    got = lax.ppermute(part, ALL, pairs)
    swapped = lax.ppermute(got, "c", [(0, 1), (1, 0)])
    other = jnp.stack([jnp.where(core == 0, got, swapped), jnp.where(core == 0, swapped, got)])
    low = jnp.where(side == 0, cross_weights, other)
    high = jnp.where(side == 0, other, cross_weights)
    return jnp.concatenate([low, high], axis=1)


def local(
    grad_out,
    t_query,
    t_key,
    t_value,
    t_out_weight,
    t_qkv_weight,
    frame_input,
    cross_weights,
    cap_key,
    cap_value,
    cap_length,
):
    samp_here, frames, patch_here, width = grad_out.shape
    slot_shape = (samp_here * frames, patch_here, width)
    core = lax.axis_index("c")
    grad_rows = grad_out.reshape(-1, width)
    halves = jnp.stack(
        [
            jnp.concatenate([t_out_weight[:, :640], t_qkv_weight[:, :1664]], axis=1),
            jnp.concatenate([t_out_weight[:, 640:], t_qkv_weight[:, 1664:]], axis=1),
        ]
    ).reshape(2, 2, -1)
    shard = lax.all_to_all(halves, "c", 0, 0)
    column = lax.all_to_all(jnp.broadcast_to(shard[None], (4,) + shard.shape), "z", 0, 0).reshape(
        72, 2 * width
    )
    cross_weights, column = lax.optimization_barrier((cross_weights, column))
    full_cross = cross_halves(cross_weights)
    out_near = gather_groups(column[:, :640], ring_groups(0))
    qkv_part, out_near = lax.optimization_barrier((column[:, 640:], out_near))
    qkv_near = gather_groups(qkv_part, ring_groups(0))
    out_whole = gather_groups(out_near, ring_groups(1))
    qkv_near, out_whole = lax.optimization_barrier((qkv_near, out_whole))
    qkv_whole = gather_groups(qkv_near, ring_groups(1))
    out_first, out_second = both_cores(out_whole)
    qkv_first, qkv_second = both_cores(qkv_whole)
    grad_heads = (
        lax.dot_general(
            grad_rows[:, :640], out_first, CONTRACT_LAST, preferred_element_type=jnp.float32
        )
        + lax.dot_general(
            grad_rows[:, 640:],
            out_second[:, :512],
            CONTRACT_LAST,
            preferred_element_type=jnp.float32,
        )
    ).astype(jnp.bfloat16)
    qkv_grad = temporal_grads(grad_heads.reshape(grad_out.shape), t_query, t_key, t_value).reshape(
        -1, 3 * width
    )
    product = (
        lax.dot_general(
            qkv_grad[:, :1664], qkv_first, CONTRACT_LAST, preferred_element_type=jnp.float32
        )
        + lax.dot_general(
            qkv_grad[:, 1664:1792],
            out_second[:, 512:],
            CONTRACT_LAST,
            preferred_element_type=jnp.float32,
        )
        + lax.dot_general(
            qkv_grad[:, 1792:], qkv_second, CONTRACT_LAST, preferred_element_type=jnp.float32
        )
    )
    mixed_rows = (grad_rows.astype(jnp.float32) + product).astype(jnp.bfloat16)
    valid_keys = jnp.arange(cap_key.shape[0]) < cap_length[0]
    arrived = lax.all_to_all(
        mixed_rows.reshape(slot_shape), SEQ, split_axis=0, concat_axis=1, tiled=True
    )
    result_rows, terms = cross_grads(
        frame_input.reshape(-1, width),
        arrived.reshape(-1, width),
        full_cross[0],
        full_cross[1],
        cap_key,
        cap_value,
        valid_keys,
    )
    grad_input = result_rows.reshape(frame_input.shape)
    chip = jnp.sum(lax.all_to_all(terms, "c", 0, 0).astype(jnp.float32), axis=0)
    head = jnp.sum(
        lax.all_to_all(chip.astype(jnp.bfloat16), ("x", "y"), 0, 0).astype(jnp.float32), axis=0
    )
    pieces = head.astype(jnp.bfloat16).reshape(1, 8, 9, -1)
    targets = jnp.where(
        jnp.arange(2)[:, None, None, None] == core, pieces, jnp.zeros_like(pieces)
    ).reshape(16, 9, -1)
    piece = jnp.sum(lax.all_to_all(targets, ("s", "z", "c"), 0, 0).astype(jnp.float32), axis=0)
    return (grad_input, piece.T)


def solution(mesh):
    fine = Mesh(mesh.devices.reshape(SHAPE), ALL)
    return jax.shard_map(
        local,
        mesh=fine,
        in_specs=(
            P("s", None, SEQ, None),
            P("s", None, SEQ, None),
            P("s", None, SEQ, None),
            P("s", None, SEQ, None),
            P(SEQ, None),
            P(SEQ, None),
            P(ALL, None, None),
            P(None, "s", None),
            P(),
            P(),
            P(),
        ),
        out_specs=(P(ALL, None, None), P(None, ALL)),
        check_vma=False,
    )
```

```python
import math

import jax
import jax.numpy as jnp
import numpy as np
from jax import lax
from jax.sharding import Mesh, PartitionSpec as P

HEADS = 16
HEAD_DIM = 72


CONTRACT_LAST = (((1,), (1,)), ((), ()))


def split_heads(tensor):
    return tensor.reshape(tensor.shape[:-1] + (HEADS, HEAD_DIM))


def merge_heads(tensor):
    return tensor.reshape(tensor.shape[:-2] + (tensor.shape[-2] * tensor.shape[-1],))


def temporal_grads(grad_heads, query, key_rows, value):
    scaling = 1.0 / math.sqrt(HEAD_DIM)
    grad_split = split_heads(grad_heads)
    query_split = split_heads(query)
    key_split = split_heads(key_rows)
    value_split = split_heads(value)
    scores = (
        jnp.einsum("sfphd,sgphd->sphfg", query_split, key_split, preferred_element_type=jnp.float32)
        * scaling
    )
    attention = jax.nn.softmax(scores, axis=-1)
    attention_low = attention.astype(jnp.bfloat16)
    value_grad = jnp.einsum(
        "sphfg,sfphd->sgphd", attention_low, grad_split, preferred_element_type=jnp.float32
    ).astype(jnp.bfloat16)
    prob_grad = jnp.einsum(
        "sfphd,sgphd->sphfg", grad_split, value_split, preferred_element_type=jnp.float32
    )
    centred = prob_grad - jnp.sum(prob_grad * attention, axis=-1, keepdims=True)
    score_grad = (attention * centred * scaling).astype(jnp.bfloat16)
    query_grad = jnp.einsum(
        "sphfg,sgphd->sfphd", score_grad, key_split, preferred_element_type=jnp.float32
    ).astype(jnp.bfloat16)
    key_grad = jnp.einsum(
        "sphfg,sfphd->sgphd", score_grad, query_split, preferred_element_type=jnp.float32
    ).astype(jnp.bfloat16)
    return jnp.concatenate(
        [merge_heads(query_grad), merge_heads(key_grad), merge_heads(value_grad)], axis=-1
    )


def cross_grads(x_rows, d_rows, place, w_query, w_out, cap_key, cap_value, valid_keys):
    scaling = 1.0 / math.sqrt(HEAD_DIM)
    cross_query = jnp.dot(x_rows, w_query, preferred_element_type=jnp.float32).astype(jnp.bfloat16)
    out_grad = lax.dot_general(
        d_rows, w_out, CONTRACT_LAST, preferred_element_type=jnp.float32
    ).astype(jnp.bfloat16)
    query_split = split_heads(cross_query)
    output_split = split_heads(out_grad)
    key_split = split_heads(cap_key)
    value_split = split_heads(cap_value)
    scores = (
        jnp.einsum("nhd,chd->nhc", query_split, key_split, preferred_element_type=jnp.float32)
        * scaling
    )
    scores = jnp.where(valid_keys[None, None, :], scores, -1e30)
    attention = jax.nn.softmax(scores, axis=-1)
    attention_low = attention.astype(jnp.bfloat16)
    prob_grad = jnp.einsum(
        "nhd,chd->nhc", output_split, value_split, preferred_element_type=jnp.float32
    )
    centred = prob_grad - jnp.sum(prob_grad * attention, axis=-1, keepdims=True)
    score_grad = (attention * centred * scaling).astype(jnp.bfloat16)
    cq_grad = merge_heads(
        jnp.einsum(
            "nhc,chd->nhd", score_grad, key_split, preferred_element_type=jnp.float32
        ).astype(jnp.bfloat16)
    )
    result = (
        jnp.dot(d_rows, place, preferred_element_type=jnp.float32)
        + lax.dot_general(cq_grad, w_query, CONTRACT_LAST, preferred_element_type=jnp.float32)
    ).astype(jnp.bfloat16)
    key_term = jnp.einsum(
        "nhc,nhd->hdc", score_grad, query_split, preferred_element_type=jnp.float32
    )
    value_term = jnp.einsum(
        "nhc,nhd->hdc", attention_low, output_split, preferred_element_type=jnp.float32
    )
    return (result, jnp.concatenate([key_term, value_term], axis=1).astype(jnp.bfloat16))


ALL = ("s", "x", "y", "z", "c")
SEQ = ("x", "y", "z", "c")
SHAPE = (2, 4, 4, 4, 2)


def flat(s, x, y, z, c):
    return (((s * 4 + x) * 4 + y) * 4 + z) * 2 + c


def ring_groups(first):
    groups = []
    for s in range(2):
        for z in range(4):
            for fixed in range(4):
                groups.append([flat(s, i, fixed, z, first) for i in range(4)])
                groups.append([flat(s, fixed, i, z, 1 - first) for i in range(4)])
    return groups


def gather_groups(block, groups):
    copies = jnp.broadcast_to(block[None], (4,) + block.shape)
    return lax.all_to_all(copies, ALL, 0, 0, axis_index_groups=groups)


def swap_cores(block):
    return lax.ppermute(block, "c", [(0, 1), (1, 0)])


def in_core_order(mine, other):
    core = lax.axis_index("c")
    return jnp.stack([jnp.where(core == 0, mine, other), jnp.where(core == 0, other, mine)])


def feature_order():
    order = np.full((2, 4, 4, 40), -1, np.int32)
    for c in range(2):
        for i in range(4):
            for j in range(4):
                x, y = (j, i) if c == 0 else (i, j)
                for q in range(36):
                    order[c, i, j, q] = 72 * (4 * x + y) + 18 * (q // 9) + 9 * c + q % 9
    return order.reshape(1280)


def cross_halves(cross_weights):
    core = lax.axis_index("c")
    side = lax.axis_index("s")

    def place(z):
        return (z % 2, z // 2)

    pairs = []
    for x in range(4):
        for y in range(4):
            for z in range(8):
                for c in range(2):
                    to = (z + (1 if c == 0 else 7)) % 8
                    s0, z0 = place(z)
                    s1, z1 = place(to)
                    pairs.append((flat(s0, x, y, z0, c), flat(s1, x, y, z1, c)))
    part = lax.dynamic_index_in_dim(cross_weights, core, 0, keepdims=False)
    got = lax.ppermute(part, ALL, pairs)
    swapped = lax.ppermute(got, "c", [(0, 1), (1, 0)])
    other = jnp.stack([jnp.where(core == 0, got, swapped), jnp.where(core == 0, swapped, got)])
    low = jnp.where(side == 0, cross_weights, other)
    high = jnp.where(side == 0, other, cross_weights)
    return jnp.concatenate([low, high], axis=1)


def local(
    grad_out,
    t_query,
    t_key,
    t_value,
    t_out_weight,
    t_qkv_weight,
    frame_input,
    cross_weights,
    cap_key,
    cap_value,
    cap_length,
):
    width = grad_out.shape[-1]
    core = lax.axis_index("c")
    grad_rows = grad_out.reshape(-1, width)
    rows = grad_rows.shape[0]
    place = (jnp.asarray(feature_order())[:, None] == jnp.arange(width)[None, :]).astype(
        jnp.bfloat16
    )
    place_mine = lax.dynamic_slice(place, (core * 640, 0), (640, width))
    grad_both = in_core_order(grad_rows, swap_cores(grad_rows)).reshape(2 * rows, width)
    shard = jnp.concatenate([t_out_weight, t_qkv_weight], axis=1).reshape(2, -1)
    column = lax.all_to_all(jnp.broadcast_to(shard[None], (4,) + shard.shape), "z", 0, 0)
    column = jnp.pad(column.reshape(36, 4 * width), ((0, 4), (0, 0)))
    cross_weights, column = lax.optimization_barrier((cross_weights, column))
    full_cross = cross_halves(cross_weights)
    near = gather_groups(column, ring_groups(0))
    out_mine = gather_groups(near[:, :, :width], ring_groups(1))
    near, out_mine = lax.optimization_barrier((near, out_mine))
    qkv_mine = gather_groups(near[:, :, width:], ring_groups(1)).reshape(640, 3 * width)
    out_mine = out_mine.reshape(640, width)
    heads_mine = (
        lax.dot_general(grad_both, out_mine, CONTRACT_LAST, preferred_element_type=jnp.float32)
        .astype(jnp.bfloat16)
        .reshape(2, rows, 640)
    )
    kept = lax.dynamic_index_in_dim(heads_mine, core, 0, keepdims=False)
    sent = lax.dynamic_index_in_dim(heads_mine, 1 - core, 0, keepdims=False)
    heads_parts = in_core_order(kept, swap_cores(sent))
    grad_heads = jnp.dot(
        jnp.concatenate([heads_parts[0], heads_parts[1]], axis=1),
        place,
        preferred_element_type=jnp.float32,
    ).astype(jnp.bfloat16)
    qkv_grad = temporal_grads(grad_heads.reshape(grad_out.shape), t_query, t_key, t_value).reshape(
        rows, 3 * width
    )
    qkv_both = in_core_order(qkv_grad, swap_cores(qkv_grad)).reshape(2 * rows, 3 * width)
    residual = lax.dot_general(
        grad_both, place_mine, CONTRACT_LAST, preferred_element_type=jnp.float32
    )
    product = lax.dot_general(
        qkv_both, qkv_mine, CONTRACT_LAST, preferred_element_type=jnp.float32
    )
    mixed = (residual + product).astype(jnp.bfloat16).reshape(2, rows, 640)
    w_out_placed = lax.dot_general(
        full_cross[1], place, CONTRACT_LAST, preferred_element_type=jnp.float32
    ).astype(jnp.bfloat16)
    valid_keys = jnp.arange(cap_key.shape[0]) < cap_length[0]
    arrived = lax.all_to_all(mixed.transpose(1, 0, 2), SEQ, split_axis=0, concat_axis=0)
    arrived = arrived.reshape(64, 2, 2, 640).transpose(0, 2, 1, 3).reshape(128, 1280)
    result_rows, terms = cross_grads(
        frame_input.reshape(-1, width),
        arrived,
        place,
        full_cross[0],
        w_out_placed,
        cap_key,
        cap_value,
        valid_keys,
    )
    grad_input = result_rows.reshape(frame_input.shape)
    head = jnp.sum(lax.all_to_all(terms, ("x", "y"), 0, 0).astype(jnp.float32), axis=0)
    pieces = head.astype(jnp.bfloat16).reshape(16, 9, -1)
    piece = jnp.sum(lax.all_to_all(pieces, ("s", "z", "c"), 0, 0).astype(jnp.float32), axis=0)
    return (grad_input, piece.T)


def solution(mesh):
    fine = Mesh(mesh.devices.reshape(SHAPE), ALL)
    return jax.shard_map(
        local,
        mesh=fine,
        in_specs=(
            P("s", None, SEQ, None),
            P("s", None, SEQ, None),
            P("s", None, SEQ, None),
            P("s", None, SEQ, None),
            P(SEQ, None),
            P(SEQ, None),
            P(ALL, None, None),
            P(None, "s", None),
            P(),
            P(),
            P(),
        ),
        out_specs=(P(ALL, None, None), P(None, ALL)),
        check_vma=False,
    )
```

```python
import math

import jax
import jax.numpy as jnp
import numpy as np
from jax import lax
from jax.experimental import pallas as pl
from jax.experimental.pallas import tpu as pltpu
from jax.sharding import Mesh, PartitionSpec as P

HEADS = 16
HEAD_DIM = 72


CONTRACT_LAST = (((1,), (1,)), ((), ()))


CONTRACT_FIRST = (((0,), (0,)), ((), ()))
SCALE = 1.0 / math.sqrt(HEAD_DIM)
CAP = 300
CAP_PAD = 384


def dot(a, b, dims=(((1,), (0,)), ((), ()))):
    return lax.dot_general(a, b, dims, preferred_element_type=jnp.float32)


def softmax(scores):
    weights = jnp.exp(scores - jnp.max(scores, axis=-1, keepdims=True))
    return weights / jnp.sum(weights, axis=-1, keepdims=True)


def score_grads(attention, prob_grad):
    centred = prob_grad - jnp.sum(prob_grad * attention, axis=-1, keepdims=True)
    return (attention * centred * SCALE).astype(jnp.bfloat16)


def temporal_kernel(grad_ref, query_ref, key_ref, value_ref, out_ref):
    rows, width = grad_ref.shape
    frames = rows // 2
    same = (lax.broadcasted_iota(jnp.int32, (rows, rows), 0) < frames) == (
        lax.broadcasted_iota(jnp.int32, (rows, rows), 1) < frames
    )
    for head in range(HEADS):
        at = slice(head * HEAD_DIM, (head + 1) * HEAD_DIM)
        grad, query, key_rows, value = (
            ref[:, at] for ref in (grad_ref, query_ref, key_ref, value_ref)
        )
        scores = jnp.where(same, dot(query, key_rows, CONTRACT_LAST) * SCALE, -jnp.inf)
        attention = softmax(scores)
        score_grad = score_grads(attention, dot(grad, value, CONTRACT_LAST))
        for part, result in enumerate(
            (
                dot(score_grad, key_rows),
                dot(score_grad, query, CONTRACT_FIRST),
                dot(attention.astype(jnp.bfloat16), grad, CONTRACT_FIRST),
            )
        ):
            start = part * width + head * HEAD_DIM
            out_ref[:, start : start + HEAD_DIM] = result.astype(jnp.bfloat16)


def temporal_grads(grad_heads, query, key_rows, value):
    rows, width = grad_heads.shape
    return pl.pallas_call(
        temporal_kernel,
        out_shape=jax.ShapeDtypeStruct((rows, 3 * width), jnp.bfloat16),
        compiler_params=pltpu.CompilerParams(vmem_limit_bytes=24 << 20),
        cost_estimate=pl.CostEstimate(
            flops=10 * rows * rows * width,
            bytes_accessed=14 * rows * width,
            transcendentals=HEADS * rows * rows,
        ),
        name="temporal_grads",
    )(grad_heads, query, key_rows, value)


def cross_kernel(
    length_ref, arrived_ref, w_out_ref, query_ref, key_ref, value_ref, cq_ref, terms_ref, og_ref
):
    og_ref[...] = dot(arrived_ref[...], w_out_ref[...]).astype(jnp.bfloat16)
    rows = query_ref.shape[0]
    valid = lax.broadcasted_iota(jnp.int32, (rows, CAP_PAD), 1) < length_ref[0]
    for head in range(HEADS):
        at = slice(head * HEAD_DIM, (head + 1) * HEAD_DIM)
        query, out_grad, key_rows, value = (
            ref[:, at] for ref in (query_ref, og_ref, key_ref, value_ref)
        )
        scores = jnp.where(valid, dot(query, key_rows, CONTRACT_LAST) * SCALE, -1e30)
        attention = softmax(scores)
        score_grad = score_grads(attention, dot(out_grad, value, CONTRACT_LAST))
        cq_ref[:, at] = dot(score_grad, key_rows).astype(jnp.bfloat16)
        key_term = dot(query, score_grad, CONTRACT_FIRST)
        value_term = dot(out_grad, attention.astype(jnp.bfloat16), CONTRACT_FIRST)
        rest = jnp.zeros((HEAD_DIM, 640 - CAP_PAD), jnp.float32)
        shifted = pltpu.roll(jnp.concatenate([value_term, rest], axis=1), CAP, 1)
        terms_ref[head] = (jnp.concatenate([key_term, rest], axis=1) + shifted).astype(
            jnp.bfloat16
        )


def cross_grads(cap_length, arrived, w_out, cross_query, cap_key, cap_value):
    rows, width = cross_query.shape
    in_vmem = pl.BlockSpec(memory_space=pltpu.VMEM)
    return pl.pallas_call(
        cross_kernel,
        in_specs=[pl.BlockSpec(memory_space=pltpu.SMEM)] + [in_vmem] * 5,
        out_specs=(in_vmem, in_vmem),
        out_shape=(
            jax.ShapeDtypeStruct((rows, width), jnp.bfloat16),
            jax.ShapeDtypeStruct((HEADS, HEAD_DIM, 640), jnp.bfloat16),
        ),
        scratch_shapes=[pltpu.VMEM((rows, width), jnp.bfloat16)],
        compiler_params=pltpu.CompilerParams(vmem_limit_bytes=32 << 20),
        cost_estimate=pl.CostEstimate(
            flops=10 * rows * CAP_PAD * width + 2 * rows * width * arrived.shape[1],
            bytes_accessed=8 << 20,
            transcendentals=HEADS * rows * CAP_PAD,
        ),
        name="cross_grads",
    )(cap_length, arrived, w_out, cross_query, cap_key, cap_value)


ALL = ("s", "x", "y", "z", "c")
SEQ = ("x", "y", "z", "c")
SHAPE = (2, 4, 4, 4, 2)


def flat(s, x, y, z, c):
    return (((s * 4 + x) * 4 + y) * 4 + z) * 2 + c


def ring_groups(first):
    groups = []
    for s in range(2):
        for z in range(4):
            for fixed in range(4):
                groups.append([flat(s, i, fixed, z, first) for i in range(4)])
                groups.append([flat(s, fixed, i, z, 1 - first) for i in range(4)])
    return groups


def gather_groups(block, groups):
    copies = jnp.broadcast_to(block[None], (4,) + block.shape)
    return lax.all_to_all(copies, ALL, 0, 0, axis_index_groups=groups)


def swap_cores(block):
    return lax.ppermute(block, "c", [(0, 1), (1, 0)])


def in_core_order(mine, other):
    core = lax.axis_index("c")
    return jnp.stack([jnp.where(core == 0, mine, other), jnp.where(core == 0, other, mine)])


def feature_order():
    order = np.full((2, 4, 4, 40), -1, np.int32)
    for c in range(2):
        for i in range(4):
            for j in range(4):
                x, y = (j, i) if c == 0 else (i, j)
                for q in range(36):
                    order[c, i, j, q] = 72 * (4 * x + y) + 18 * (q // 9) + 9 * c + q % 9
    return order.reshape(1280)


def cross_halves(cross_weights):
    core = lax.axis_index("c")
    side = lax.axis_index("s")

    def place(z):
        return (z % 2, z // 2)

    pairs = []
    for x in range(4):
        for y in range(4):
            for z in range(8):
                for c in range(2):
                    to = (z + (1 if c == 0 else 7)) % 8
                    s0, z0 = place(z)
                    s1, z1 = place(to)
                    pairs.append((flat(s0, x, y, z0, c), flat(s1, x, y, z1, c)))
    part = lax.dynamic_index_in_dim(cross_weights, core, 0, keepdims=False)
    got = lax.ppermute(part, ALL, pairs)
    swapped = lax.ppermute(got, "c", [(0, 1), (1, 0)])
    other = jnp.stack([jnp.where(core == 0, got, swapped), jnp.where(core == 0, swapped, got)])
    low = jnp.where(side == 0, cross_weights, other)
    high = jnp.where(side == 0, other, cross_weights)
    return jnp.concatenate([low, high], axis=1)


def local(
    grad_out,
    t_query,
    t_key,
    t_value,
    t_out_weight,
    t_qkv_weight,
    frame_input,
    cross_weights,
    cap_key,
    cap_value,
    cap_length,
):
    width = grad_out.shape[-1]
    core = lax.axis_index("c")
    grad_rows = grad_out.reshape(-1, width)
    rows = grad_rows.shape[0]
    place = (jnp.asarray(feature_order())[:, None] == jnp.arange(width)[None, :]).astype(
        jnp.bfloat16
    )
    place_mine = lax.dynamic_slice(place, (core * 640, 0), (640, width))
    grad_both = in_core_order(grad_rows, swap_cores(grad_rows)).reshape(2 * rows, width)
    shard = jnp.concatenate([t_out_weight, t_qkv_weight], axis=1).reshape(2, -1)
    column = lax.all_to_all(jnp.broadcast_to(shard[None], (4,) + shard.shape), "z", 0, 0)
    column = jnp.pad(column.reshape(36, 4 * width), ((0, 4), (0, 0)))
    near = gather_groups(column, ring_groups(0))
    out_mine = gather_groups(near[:, :, :width], ring_groups(1))
    near, out_mine, cross_weights = lax.optimization_barrier((near, out_mine, cross_weights))
    full_cross = cross_halves(cross_weights)
    qkv_mine = gather_groups(near[:, :, width:], ring_groups(1)).reshape(640, 3 * width)
    out_mine = out_mine.reshape(640, width)
    heads_mine = (
        lax.dot_general(grad_both, out_mine, CONTRACT_LAST, preferred_element_type=jnp.float32)
        .astype(jnp.bfloat16)
        .reshape(2, rows, 640)
    )
    kept = lax.dynamic_index_in_dim(heads_mine, core, 0, keepdims=False)
    sent = lax.dynamic_index_in_dim(heads_mine, 1 - core, 0, keepdims=False)
    heads_parts = in_core_order(kept, swap_cores(sent))
    grad_heads = jnp.dot(
        jnp.concatenate([heads_parts[0], heads_parts[1]], axis=1),
        place,
        preferred_element_type=jnp.float32,
    ).astype(jnp.bfloat16)
    qkv_grad = temporal_grads(
        grad_heads, *(saved.reshape(rows, width) for saved in (t_query, t_key, t_value))
    )
    qkv_both = in_core_order(qkv_grad, swap_cores(qkv_grad)).reshape(2 * rows, 3 * width)
    residual = lax.dot_general(
        grad_both, place_mine, CONTRACT_LAST, preferred_element_type=jnp.float32
    )
    product = lax.dot_general(
        qkv_both, qkv_mine, CONTRACT_LAST, preferred_element_type=jnp.float32
    )
    mixed = (residual + product).astype(jnp.bfloat16).reshape(2, rows, 640)
    w_out_placed = lax.dot_general(
        place, full_cross[1], CONTRACT_LAST, preferred_element_type=jnp.float32
    ).astype(jnp.bfloat16)
    cross_query = jnp.dot(
        frame_input.reshape(rows, width), full_cross[0], preferred_element_type=jnp.float32
    ).astype(jnp.bfloat16)
    padding = ((0, CAP_PAD - CAP), (0, 0))
    arrived = lax.all_to_all(mixed.transpose(1, 0, 2), SEQ, split_axis=0, concat_axis=0)
    arrived = arrived.reshape(64, 2, 2, 640).transpose(0, 2, 1, 3).reshape(128, 1280)
    cq_grad, terms = cross_grads(
        cap_length,
        arrived,
        w_out_placed,
        cross_query,
        jnp.pad(cap_key, padding),
        jnp.pad(cap_value, padding),
    )
    grad_input = (
        jnp.dot(arrived, place, preferred_element_type=jnp.float32)
        + lax.dot_general(cq_grad, full_cross[0], CONTRACT_LAST, preferred_element_type=jnp.float32)
    ).astype(jnp.bfloat16)
    head = jnp.sum(lax.all_to_all(terms, ("x", "y"), 0, 0).astype(jnp.float32), axis=0)
    head = head.astype(jnp.bfloat16)
    pieces = jnp.concatenate(
        [head[:, :CAP].reshape(8, 9, CAP), head[:, CAP : 2 * CAP].reshape(8, 9, CAP)]
    )
    piece = jnp.sum(lax.all_to_all(pieces, ("s", "z", "c"), 0, 0).astype(jnp.float32), axis=0)
    return (grad_input.reshape(frame_input.shape), piece.T)


def solution(mesh):
    fine = Mesh(mesh.devices.reshape(SHAPE), ALL)
    return jax.shard_map(
        local,
        mesh=fine,
        in_specs=(
            P("s", None, SEQ, None),
            P("s", None, SEQ, None),
            P("s", None, SEQ, None),
            P("s", None, SEQ, None),
            P(SEQ, None),
            P(SEQ, None),
            P(ALL, None, None),
            P(None, "s", None),
            P(),
            P(),
            P(),
        ),
        out_specs=(P(ALL, None, None), P(None, ALL)),
        check_vma=False,
    )
```

```python
import math

import jax
import jax.numpy as jnp
import numpy as np
from jax import lax
from jax.experimental import pallas as pl
from jax.experimental.pallas import tpu as pltpu
from jax.sharding import Mesh, PartitionSpec as P

HEADS = 16
HEAD_DIM = 72


CONTRACT_LAST = (((1,), (1,)), ((), ()))


CONTRACT_FIRST = (((0,), (0,)), ((), ()))
SCALE = 1.0 / math.sqrt(HEAD_DIM)
CAP = 300
CAP_PAD = 384


def dot(a, b, dims=(((1,), (0,)), ((), ()))):
    return lax.dot_general(a, b, dims, preferred_element_type=jnp.float32)


def softmax(scores):
    weights = jnp.exp(scores - jnp.max(scores, axis=-1, keepdims=True))
    return weights / jnp.sum(weights, axis=-1, keepdims=True)


def score_grads(attention, prob_grad):
    centred = prob_grad - jnp.sum(prob_grad * attention, axis=-1, keepdims=True)
    return (attention * centred * SCALE).astype(jnp.bfloat16)


def temporal_kernel(grad_ref, query_ref, key_ref, value_ref, out_ref):
    rows, width = grad_ref.shape
    frames = rows // 2
    same = (lax.broadcasted_iota(jnp.int32, (rows, rows), 0) < frames) == (
        lax.broadcasted_iota(jnp.int32, (rows, rows), 1) < frames
    )
    for head in range(HEADS):
        at = slice(head * HEAD_DIM, (head + 1) * HEAD_DIM)
        grad, query, key_rows, value = (
            ref[:, at] for ref in (grad_ref, query_ref, key_ref, value_ref)
        )
        scores = jnp.where(same, dot(query, key_rows, CONTRACT_LAST) * SCALE, -jnp.inf)
        attention = softmax(scores)
        score_grad = score_grads(attention, dot(grad, value, CONTRACT_LAST))
        for part, result in enumerate(
            (
                dot(score_grad, key_rows),
                dot(score_grad, query, CONTRACT_FIRST),
                dot(attention.astype(jnp.bfloat16), grad, CONTRACT_FIRST),
            )
        ):
            start = part * width + head * HEAD_DIM
            out_ref[:, start : start + HEAD_DIM] = result.astype(jnp.bfloat16)


def temporal_grads(grad_heads, query, key_rows, value):
    rows, width = grad_heads.shape
    return pl.pallas_call(
        temporal_kernel,
        out_shape=jax.ShapeDtypeStruct((rows, 3 * width), jnp.bfloat16),
        compiler_params=pltpu.CompilerParams(vmem_limit_bytes=24 << 20),
        cost_estimate=pl.CostEstimate(
            flops=10 * rows * rows * width,
            bytes_accessed=14 * rows * width,
            transcendentals=HEADS * rows * rows,
        ),
        name="temporal_grads",
    )(grad_heads, query, key_rows, value)


def mixed_kernel(slot_ref, qkv_ref, residual_ref, w0, w1, w2, w3, out_ref, held, arrived):
    copies = [
        pltpu.make_async_copy(block, held.at[slot_ref[i]], arrived.at[i])
        for i, block in enumerate((w0, w1, w2, w3))
    ]
    for copy in copies:
        copy.start()
    for copy in copies:
        copy.wait()
    weight = held[...].reshape(-1, held.shape[2])
    product = dot(qkv_ref[...], weight, CONTRACT_LAST)
    out_ref[...] = (residual_ref[...] + product).astype(jnp.bfloat16)


def mixed_half(slots, qkv_both, residual, blocks):
    in_vmem = pl.BlockSpec(memory_space=pltpu.VMEM)
    return pl.pallas_call(
        mixed_kernel,
        in_specs=[pl.BlockSpec(memory_space=pltpu.SMEM), in_vmem, in_vmem]
        + [pl.BlockSpec(memory_space=pl.ANY)] * 4,
        out_specs=in_vmem,
        out_shape=jax.ShapeDtypeStruct(residual.shape, jnp.bfloat16),
        scratch_shapes=[
            pltpu.VMEM((4,) + blocks[0].shape, jnp.bfloat16),
            pltpu.SemaphoreType.DMA((4,)),
        ],
        compiler_params=pltpu.CompilerParams(vmem_limit_bytes=32 << 20),
        cost_estimate=pl.CostEstimate(
            flops=2 * residual.size * qkv_both.shape[1], bytes_accessed=8 << 20, transcendentals=0
        ),
        name="mixed_half",
    )(slots, qkv_both, residual, *blocks)


def cross_kernel(
    length_ref, arrived_ref, w_out_ref, query_ref, key_ref, value_ref, cq_ref, terms_ref, og_ref
):
    og_ref[...] = dot(arrived_ref[...], w_out_ref[...]).astype(jnp.bfloat16)
    rows = query_ref.shape[0]
    valid = lax.broadcasted_iota(jnp.int32, (rows, CAP_PAD), 1) < length_ref[0]
    for head in range(HEADS):
        at = slice(head * HEAD_DIM, (head + 1) * HEAD_DIM)
        query, out_grad, key_rows, value = (
            ref[:, at] for ref in (query_ref, og_ref, key_ref, value_ref)
        )
        scores = jnp.where(valid, dot(query, key_rows, CONTRACT_LAST) * SCALE, -1e30)
        attention = softmax(scores)
        score_grad = score_grads(attention, dot(out_grad, value, CONTRACT_LAST))
        cq_ref[:, at] = dot(score_grad, key_rows).astype(jnp.bfloat16)
        key_term = dot(query, score_grad, CONTRACT_FIRST)
        value_term = dot(out_grad, attention.astype(jnp.bfloat16), CONTRACT_FIRST)
        rest = jnp.zeros((HEAD_DIM, 640 - CAP_PAD), jnp.float32)
        shifted = pltpu.roll(jnp.concatenate([value_term, rest], axis=1), CAP, 1)
        terms_ref[head] = (jnp.concatenate([key_term, rest], axis=1) + shifted).astype(
            jnp.bfloat16
        )


def cross_grads(cap_length, arrived, w_out, cross_query, cap_key, cap_value):
    rows, width = cross_query.shape
    in_vmem = pl.BlockSpec(memory_space=pltpu.VMEM)
    return pl.pallas_call(
        cross_kernel,
        in_specs=[pl.BlockSpec(memory_space=pltpu.SMEM)] + [in_vmem] * 5,
        out_specs=(in_vmem, in_vmem),
        out_shape=(
            jax.ShapeDtypeStruct((rows, width), jnp.bfloat16),
            jax.ShapeDtypeStruct((HEADS, HEAD_DIM, 640), jnp.bfloat16),
        ),
        scratch_shapes=[pltpu.VMEM((rows, width), jnp.bfloat16)],
        compiler_params=pltpu.CompilerParams(vmem_limit_bytes=32 << 20),
        cost_estimate=pl.CostEstimate(
            flops=10 * rows * CAP_PAD * width + 2 * rows * width * arrived.shape[1],
            bytes_accessed=8 << 20,
            transcendentals=HEADS * rows * CAP_PAD,
        ),
        name="cross_grads",
    )(cap_length, arrived, w_out, cross_query, cap_key, cap_value)


ALL = ("s", "x", "y", "z", "c")
SEQ = ("x", "y", "z", "c")
SHAPE = (2, 4, 4, 4, 2)


def flat(s, x, y, z, c):
    return (((s * 4 + x) * 4 + y) * 4 + z) * 2 + c


def ring_groups(first):
    groups = []
    for s in range(2):
        for z in range(4):
            for fixed in range(4):
                groups.append([flat(s, i, fixed, z, first) for i in range(4)])
                groups.append([flat(s, fixed, i, z, 1 - first) for i in range(4)])
    return groups


def gather_groups(block, groups):
    copies = jnp.broadcast_to(block[None], (4,) + block.shape)
    return lax.all_to_all(copies, ALL, 0, 0, axis_index_groups=groups)


def shift_last(block, step):
    pairs = []
    for s in range(2):
        for x in range(4):
            for y in range(4):
                for z in range(4):
                    pairs.append((flat(s, x, y, z, 0), flat(s, x, (y + step) % 4, z, 0)))
                    pairs.append((flat(s, x, y, z, 1), flat(s, (x + step) % 4, y, z, 1)))
    return lax.ppermute(block, ALL, pairs)


def swap_cores(block):
    return lax.ppermute(block, "c", [(0, 1), (1, 0)])


def in_core_order(mine, other):
    core = lax.axis_index("c")
    return jnp.stack([jnp.where(core == 0, mine, other), jnp.where(core == 0, other, mine)])


def feature_order():
    order = np.full((2, 4, 4, 40), -1, np.int32)
    for c in range(2):
        for i in range(4):
            for j in range(4):
                x, y = (j, i) if c == 0 else (i, j)
                for q in range(36):
                    order[c, i, j, q] = 72 * (4 * x + y) + 18 * (q // 9) + 9 * c + q % 9
    return order.reshape(1280)


def cross_halves(cross_weights):
    core = lax.axis_index("c")
    side = lax.axis_index("s")

    def place(z):
        return (z % 2, z // 2)

    pairs = []
    for x in range(4):
        for y in range(4):
            for z in range(8):
                for c in range(2):
                    to = (z + (1 if c == 0 else 7)) % 8
                    s0, z0 = place(z)
                    s1, z1 = place(to)
                    pairs.append((flat(s0, x, y, z0, c), flat(s1, x, y, z1, c)))
    part = lax.dynamic_index_in_dim(cross_weights, core, 0, keepdims=False)
    got = lax.ppermute(part, ALL, pairs)
    swapped = lax.ppermute(got, "c", [(0, 1), (1, 0)])
    other = jnp.stack([jnp.where(core == 0, got, swapped), jnp.where(core == 0, swapped, got)])
    low = jnp.where(side == 0, cross_weights, other)
    high = jnp.where(side == 0, other, cross_weights)
    return jnp.concatenate([low, high], axis=1)


def local(
    grad_out,
    t_query,
    t_key,
    t_value,
    t_out_weight,
    t_qkv_weight,
    frame_input,
    cross_weights,
    cap_key,
    cap_value,
    cap_length,
):
    width = grad_out.shape[-1]
    core = lax.axis_index("c")
    grad_rows = grad_out.reshape(-1, width)
    rows = grad_rows.shape[0]
    place = (jnp.asarray(feature_order())[:, None] == jnp.arange(width)[None, :]).astype(
        jnp.bfloat16
    )
    place_mine = lax.dynamic_slice(place, (core * 640, 0), (640, width))
    grad_both = in_core_order(grad_rows, swap_cores(grad_rows)).reshape(2 * rows, width)
    shard = jnp.concatenate([t_out_weight, t_qkv_weight], axis=1).reshape(2, -1)
    column = lax.all_to_all(jnp.broadcast_to(shard[None], (4,) + shard.shape), "z", 0, 0)
    column = jnp.pad(column.reshape(36, 4 * width), ((0, 4), (0, 0)))
    near = gather_groups(column, ring_groups(0))
    near, cross_weights = lax.optimization_barrier((near, cross_weights))
    qkv_near = near[:, :, width:].reshape(160, 3 * width)
    blocks = [qkv_near] + [shift_last(qkv_near, step) for step in (1, 3, 2)]
    place_here = jnp.where(core == 0, lax.axis_index("y"), lax.axis_index("x"))
    slots = (place_here - jnp.array([0, 1, 3, 2], jnp.int32)) % 4
    out_mine = gather_groups(near[:, :, :width], ring_groups(1)).reshape(640, width)
    full_cross = cross_halves(cross_weights)
    heads_mine = (
        lax.dot_general(grad_both, out_mine, CONTRACT_LAST, preferred_element_type=jnp.float32)
        .astype(jnp.bfloat16)
        .reshape(2, rows, 640)
    )
    kept = lax.dynamic_index_in_dim(heads_mine, core, 0, keepdims=False)
    sent = lax.dynamic_index_in_dim(heads_mine, 1 - core, 0, keepdims=False)
    heads_parts = in_core_order(kept, swap_cores(sent))
    grad_heads = jnp.dot(
        jnp.concatenate([heads_parts[0], heads_parts[1]], axis=1),
        place,
        preferred_element_type=jnp.float32,
    ).astype(jnp.bfloat16)
    qkv_grad = temporal_grads(
        grad_heads, *(saved.reshape(rows, width) for saved in (t_query, t_key, t_value))
    )
    qkv_both = in_core_order(qkv_grad, swap_cores(qkv_grad)).reshape(2 * rows, 3 * width)
    residual = lax.dot_general(
        grad_both, place_mine, CONTRACT_LAST, preferred_element_type=jnp.float32
    )
    mixed = mixed_half(slots, qkv_both, residual, blocks).reshape(2, rows, 640)
    w_out_placed = lax.dot_general(
        place, full_cross[1], CONTRACT_LAST, preferred_element_type=jnp.float32
    ).astype(jnp.bfloat16)
    cross_query = jnp.dot(
        frame_input.reshape(rows, width), full_cross[0], preferred_element_type=jnp.float32
    ).astype(jnp.bfloat16)
    padding = ((0, CAP_PAD - CAP), (0, 0))
    arrived = lax.all_to_all(mixed.transpose(1, 0, 2), SEQ, split_axis=0, concat_axis=0)
    arrived = arrived.reshape(64, 2, 2, 640).transpose(0, 2, 1, 3).reshape(128, 1280)
    cq_grad, terms = cross_grads(
        cap_length,
        arrived,
        w_out_placed,
        cross_query,
        jnp.pad(cap_key, padding),
        jnp.pad(cap_value, padding),
    )
    grad_input = (
        jnp.dot(arrived, place, preferred_element_type=jnp.float32)
        + lax.dot_general(cq_grad, full_cross[0], CONTRACT_LAST, preferred_element_type=jnp.float32)
    ).astype(jnp.bfloat16)
    head = jnp.sum(lax.all_to_all(terms, ("x", "y"), 0, 0).astype(jnp.float32), axis=0)
    head = head.astype(jnp.bfloat16)
    pieces = jnp.concatenate(
        [head[:, :CAP].reshape(8, 9, CAP), head[:, CAP : 2 * CAP].reshape(8, 9, CAP)]
    )
    piece = jnp.sum(lax.all_to_all(pieces, ("s", "z", "c"), 0, 0).astype(jnp.float32), axis=0)
    return (grad_input.reshape(frame_input.shape), piece.T)


def solution(mesh):
    fine = Mesh(mesh.devices.reshape(SHAPE), ALL)
    return jax.shard_map(
        local,
        mesh=fine,
        in_specs=(
            P("s", None, SEQ, None),
            P("s", None, SEQ, None),
            P("s", None, SEQ, None),
            P("s", None, SEQ, None),
            P(SEQ, None),
            P(SEQ, None),
            P(ALL, None, None),
            P(None, "s", None),
            P(),
            P(),
            P(),
        ),
        out_specs=(P(ALL, None, None), P(None, ALL)),
        check_vma=False,
    )
```

```python
import math

import jax
import jax.numpy as jnp
import numpy as np
from jax import lax
from jax.experimental import pallas as pl
from jax.experimental.pallas import tpu as pltpu
from jax.sharding import Mesh, PartitionSpec as P

HEADS = 16
HEAD_DIM = 72


CONTRACT_LAST = (((1,), (1,)), ((), ()))


CONTRACT_FIRST = (((0,), (0,)), ((), ()))
SCALE = 1.0 / math.sqrt(HEAD_DIM)
CAP = 300
CAP_PAD = 384


def dot(a, b, dims=(((1,), (0,)), ((), ()))):
    return lax.dot_general(a, b, dims, preferred_element_type=jnp.float32)


def softmax(scores):
    weights = jnp.exp(scores - jnp.max(scores, axis=-1, keepdims=True))
    return weights / jnp.sum(weights, axis=-1, keepdims=True)


def score_grads(attention, prob_grad):
    centred = prob_grad - jnp.sum(prob_grad * attention, axis=-1, keepdims=True)
    return (attention * centred * SCALE).astype(jnp.bfloat16)


def temporal_kernel(grad_ref, query_ref, key_ref, value_ref, out_ref):
    rows, width = grad_ref.shape
    frames = rows // 2
    same = (lax.broadcasted_iota(jnp.int32, (rows, rows), 0) < frames) == (
        lax.broadcasted_iota(jnp.int32, (rows, rows), 1) < frames
    )
    for head in range(HEADS):
        at = slice(head * HEAD_DIM, (head + 1) * HEAD_DIM)
        grad, query, key_rows, value = (
            ref[:, at] for ref in (grad_ref, query_ref, key_ref, value_ref)
        )
        scores = jnp.where(same, dot(query, key_rows, CONTRACT_LAST) * SCALE, -jnp.inf)
        attention = softmax(scores)
        score_grad = score_grads(attention, dot(grad, value, CONTRACT_LAST))
        for part, result in enumerate(
            (
                dot(score_grad, key_rows),
                dot(score_grad, query, CONTRACT_FIRST),
                dot(attention.astype(jnp.bfloat16), grad, CONTRACT_FIRST),
            )
        ):
            start = part * width + head * HEAD_DIM
            out_ref[:, start : start + HEAD_DIM] = result.astype(jnp.bfloat16)


def temporal_grads(grad_heads, query, key_rows, value):
    rows, width = grad_heads.shape
    return pl.pallas_call(
        temporal_kernel,
        out_shape=jax.ShapeDtypeStruct((rows, 3 * width), jnp.bfloat16),
        compiler_params=pltpu.CompilerParams(vmem_limit_bytes=24 << 20),
        cost_estimate=pl.CostEstimate(
            flops=rows * width, bytes_accessed=2 * rows * width, transcendentals=0
        ),
        name="temporal_grads",
    )(grad_heads, query, key_rows, value)


def mixed_kernel(slot_ref, qkv_ref, residual_ref, w0, w1, w2, w3, out_ref, held, arrived):
    copies = [
        pltpu.make_async_copy(block, held.at[slot_ref[i]], arrived.at[i])
        for i, block in enumerate((w0, w1, w2, w3))
    ]
    for copy in copies:
        copy.start()
    for copy in copies:
        copy.wait()
    weight = held[...].reshape(-1, held.shape[2])
    product = dot(qkv_ref[...], weight, CONTRACT_LAST)
    out_ref[...] = (residual_ref[...] + product).astype(jnp.bfloat16)


def mixed_half(slots, qkv_both, residual, blocks):
    in_vmem = pl.BlockSpec(memory_space=pltpu.VMEM)
    return pl.pallas_call(
        mixed_kernel,
        in_specs=[pl.BlockSpec(memory_space=pltpu.SMEM), in_vmem, in_vmem]
        + [pl.BlockSpec(memory_space=pl.ANY)] * 4,
        out_specs=in_vmem,
        out_shape=jax.ShapeDtypeStruct(residual.shape, jnp.bfloat16),
        scratch_shapes=[
            pltpu.VMEM((4,) + blocks[0].shape, jnp.bfloat16),
            pltpu.SemaphoreType.DMA((4,)),
        ],
        compiler_params=pltpu.CompilerParams(vmem_limit_bytes=32 << 20),
        cost_estimate=pl.CostEstimate(
            flops=2 * residual.size * qkv_both.shape[1], bytes_accessed=8 << 20, transcendentals=0
        ),
        name="mixed_half",
    )(slots, qkv_both, residual, *blocks)


def probs_kernel(length_ref, query_ref, key_ref, probs_ref):
    rows = query_ref.shape[0]
    valid = lax.broadcasted_iota(jnp.int32, (rows, CAP_PAD), 1) < length_ref[0]
    for head in range(HEADS):
        at = slice(head * HEAD_DIM, (head + 1) * HEAD_DIM)
        scores = dot(query_ref[:, at], key_ref[:, at], CONTRACT_LAST) * SCALE
        probs_ref[head] = softmax(jnp.where(valid, scores, -1e30))


def cross_probs(cap_length, cross_query, cap_key):
    rows, width = cross_query.shape
    in_vmem = pl.BlockSpec(memory_space=pltpu.VMEM)
    return pl.pallas_call(
        probs_kernel,
        in_specs=[pl.BlockSpec(memory_space=pltpu.SMEM), in_vmem, in_vmem],
        out_specs=in_vmem,
        out_shape=jax.ShapeDtypeStruct((HEADS, rows, CAP_PAD), jnp.float32),
        compiler_params=pltpu.CompilerParams(vmem_limit_bytes=16 << 20),
        cost_estimate=pl.CostEstimate(
            flops=2 * rows * CAP_PAD * width,
            bytes_accessed=4 << 20,
            transcendentals=HEADS * rows * CAP_PAD,
        ),
        name="cross_probs",
    )(cap_length, cross_query, cap_key)


def cross_kernel(
    core_ref,
    arrived_ref,
    w_out_ref,
    query_ref,
    key_ref,
    value_ref,
    probs_ref,
    cq_ref,
    keep_ref,
    send_ref,
    og_ref,
):
    og_ref[...] = dot(arrived_ref[...], w_out_ref[...]).astype(jnp.bfloat16)
    first = core_ref[0] == 0
    for head in range(HEADS):
        at = slice(head * HEAD_DIM, (head + 1) * HEAD_DIM)
        query, out_grad, key_rows, value = (
            ref[:, at] for ref in (query_ref, og_ref, key_ref, value_ref)
        )
        attention = probs_ref[head]
        score_grad = score_grads(attention, dot(out_grad, value, CONTRACT_LAST))
        cq_ref[:, at] = dot(score_grad, key_rows).astype(jnp.bfloat16)
        key_term = dot(query, score_grad, CONTRACT_FIRST)
        value_term = dot(out_grad, attention.astype(jnp.bfloat16), CONTRACT_FIRST)
        keep_ref[head] = jnp.where(first, key_term, value_term).astype(jnp.bfloat16)
        send_ref[head] = jnp.where(first, value_term, key_term).astype(jnp.bfloat16)


def cross_grads(core, arrived, w_out, cross_query, cap_key, cap_value, probs):
    rows, width = cross_query.shape
    in_vmem = pl.BlockSpec(memory_space=pltpu.VMEM)
    term = jax.ShapeDtypeStruct((HEADS, HEAD_DIM, CAP_PAD), jnp.bfloat16)
    return pl.pallas_call(
        cross_kernel,
        in_specs=[pl.BlockSpec(memory_space=pltpu.SMEM)] + [in_vmem] * 6,
        out_specs=(in_vmem,) * 3,
        out_shape=(jax.ShapeDtypeStruct((rows, width), jnp.bfloat16), term, term),
        scratch_shapes=[pltpu.VMEM((rows, width), jnp.bfloat16)],
        compiler_params=pltpu.CompilerParams(vmem_limit_bytes=32 << 20),
        cost_estimate=pl.CostEstimate(
            flops=8 * rows * CAP_PAD * width + 2 * rows * width * arrived.shape[1],
            bytes_accessed=12 << 20,
            transcendentals=0,
        ),
        name="cross_grads",
    )(core, arrived, w_out, cross_query, cap_key, cap_value, probs)


ALL = ("s", "x", "y", "z", "c")
SEQ = ("x", "y", "z", "c")
SHAPE = (2, 4, 4, 4, 2)


def flat(s, x, y, z, c):
    return (((s * 4 + x) * 4 + y) * 4 + z) * 2 + c


def ring_groups(first):
    groups = []
    for s in range(2):
        for z in range(4):
            for fixed in range(4):
                groups.append([flat(s, i, fixed, z, first) for i in range(4)])
                groups.append([flat(s, fixed, i, z, 1 - first) for i in range(4)])
    return groups


def gather_groups(block, groups):
    copies = jnp.broadcast_to(block[None], (4,) + block.shape)
    return lax.all_to_all(copies, ALL, 0, 0, axis_index_groups=groups)


def shift_last(block, step):
    pairs = []
    for s in range(2):
        for x in range(4):
            for y in range(4):
                for z in range(4):
                    pairs.append((flat(s, x, y, z, 0), flat(s, x, (y + step) % 4, z, 0)))
                    pairs.append((flat(s, x, y, z, 1), flat(s, (x + step) % 4, y, z, 1)))
    return lax.ppermute(block, ALL, pairs)


def swap_cores(block):
    return lax.ppermute(block, "c", [(0, 1), (1, 0)])


def in_core_order(mine, other):
    core = lax.axis_index("c")
    return jnp.stack([jnp.where(core == 0, mine, other), jnp.where(core == 0, other, mine)])


def feature_order():
    order = np.full((2, 4, 4, 40), -1, np.int32)
    for c in range(2):
        for i in range(4):
            for j in range(4):
                x, y = (j, i) if c == 0 else (i, j)
                for q in range(36):
                    order[c, i, j, q] = 72 * (4 * x + y) + 18 * (q // 9) + 9 * c + q % 9
    return order.reshape(1280)


def cross_halves(cross_weights):
    core = lax.axis_index("c")
    side = lax.axis_index("s")

    def place(z):
        return (z % 2, z // 2)

    pairs = []
    for x in range(4):
        for y in range(4):
            for z in range(8):
                for c in range(2):
                    to = (z + (1 if c == 0 else 7)) % 8
                    s0, z0 = place(z)
                    s1, z1 = place(to)
                    pairs.append((flat(s0, x, y, z0, c), flat(s1, x, y, z1, c)))
    part = lax.dynamic_index_in_dim(cross_weights, core, 0, keepdims=False)
    got = lax.ppermute(part, ALL, pairs)
    swapped = lax.ppermute(got, "c", [(0, 1), (1, 0)])
    other = jnp.stack([jnp.where(core == 0, got, swapped), jnp.where(core == 0, swapped, got)])
    low = jnp.where(side == 0, cross_weights, other)
    high = jnp.where(side == 0, other, cross_weights)
    return jnp.concatenate([low, high], axis=1)


def local(
    grad_out,
    t_query,
    t_key,
    t_value,
    t_out_weight,
    t_qkv_weight,
    frame_input,
    cross_weights,
    cap_key,
    cap_value,
    cap_length,
):
    width = grad_out.shape[-1]
    core = lax.axis_index("c")
    grad_rows = grad_out.reshape(-1, width)
    rows = grad_rows.shape[0]
    place = (jnp.asarray(feature_order())[:, None] == jnp.arange(width)[None, :]).astype(
        jnp.bfloat16
    )
    place_mine = lax.dynamic_slice(place, (core * 640, 0), (640, width))
    grad_both = in_core_order(grad_rows, swap_cores(grad_rows)).reshape(2 * rows, width)
    shard = jnp.concatenate([t_out_weight, t_qkv_weight], axis=1).reshape(2, -1)
    column = lax.all_to_all(jnp.broadcast_to(shard[None], (4,) + shard.shape), "z", 0, 0)
    column = jnp.pad(column.reshape(36, 4 * width), ((0, 4), (0, 0)))
    near = gather_groups(column, ring_groups(0))
    near, cross_weights = lax.optimization_barrier((near, cross_weights))
    qkv_near = near[:, :, width:].reshape(160, 3 * width)
    blocks = [qkv_near] + [shift_last(qkv_near, step) for step in (1, 3, 2)]
    place_here = jnp.where(core == 0, lax.axis_index("y"), lax.axis_index("x"))
    slots = (place_here - jnp.array([0, 1, 3, 2], jnp.int32)) % 4
    out_mine = gather_groups(near[:, :, :width], ring_groups(1)).reshape(640, width)
    full_cross = cross_halves(cross_weights)
    residual = lax.dot_general(
        grad_both, place_mine, CONTRACT_LAST, preferred_element_type=jnp.float32
    )
    padding = ((0, CAP_PAD - CAP), (0, 0))
    cap_key, cap_value = jnp.pad(cap_key, padding), jnp.pad(cap_value, padding)
    out_mine, residual, place, cap_key, cap_value = lax.optimization_barrier(
        (out_mine, residual, place, cap_key, cap_value)
    )
    heads_mine = (
        lax.dot_general(grad_both, out_mine, CONTRACT_LAST, preferred_element_type=jnp.float32)
        .astype(jnp.bfloat16)
        .reshape(2, rows, 640)
    )
    kept = lax.dynamic_index_in_dim(heads_mine, core, 0, keepdims=False)
    sent = lax.dynamic_index_in_dim(heads_mine, 1 - core, 0, keepdims=False)
    heads_parts = in_core_order(kept, swap_cores(sent))
    grad_heads = jnp.dot(
        jnp.concatenate([heads_parts[0], heads_parts[1]], axis=1),
        place,
        preferred_element_type=jnp.float32,
    ).astype(jnp.bfloat16)
    qkv_grad = temporal_grads(
        grad_heads, *(saved.reshape(rows, width) for saved in (t_query, t_key, t_value))
    )
    qkv_grad, *blocks = lax.optimization_barrier((qkv_grad, *blocks))
    qkv_both = in_core_order(qkv_grad, swap_cores(qkv_grad)).reshape(2 * rows, 3 * width)
    mixed = mixed_half(slots, qkv_both, residual, blocks).reshape(2, rows, 640)
    w_out_placed = lax.dot_general(
        place, full_cross[1], CONTRACT_LAST, preferred_element_type=jnp.float32
    ).astype(jnp.bfloat16)
    cross_query = jnp.dot(
        frame_input.reshape(rows, width), full_cross[0], preferred_element_type=jnp.float32
    ).astype(jnp.bfloat16)
    probs = cross_probs(cap_length, cross_query, cap_key)
    arrived = lax.all_to_all(mixed.transpose(1, 0, 2), SEQ, split_axis=0, concat_axis=0)
    arrived = arrived.reshape(64, 2, 2, 640).transpose(0, 2, 1, 3).reshape(128, 1280)
    cq_grad, keep, send = cross_grads(
        core.reshape(1), arrived, w_out_placed, cross_query, cap_key, cap_value, probs
    )
    chip = (keep.astype(jnp.float32) + swap_cores(send).astype(jnp.float32)).astype(jnp.bfloat16)
    grad_input = (
        jnp.dot(arrived, place, preferred_element_type=jnp.float32)
        + lax.dot_general(cq_grad, full_cross[0], CONTRACT_LAST, preferred_element_type=jnp.float32)
    ).astype(jnp.bfloat16)
    head = jnp.sum(lax.all_to_all(chip, ("x", "y"), 0, 0).astype(jnp.float32), axis=0)
    pieces = head[:, :CAP].astype(jnp.bfloat16).reshape(1, 8, 9, CAP)
    sides = jnp.arange(2).reshape(2, 1, 1, 1) == core
    pieces = jnp.where(sides, pieces, jnp.zeros_like(pieces)).reshape(16, 9, CAP)
    piece = jnp.sum(lax.all_to_all(pieces, ("s", "z", "c"), 0, 0).astype(jnp.float32), axis=0)
    return (grad_input.reshape(frame_input.shape), piece.T)


def solution(mesh):
    fine = Mesh(mesh.devices.reshape(SHAPE), ALL)
    return jax.shard_map(
        local,
        mesh=fine,
        in_specs=(
            P("s", None, SEQ, None),
            P("s", None, SEQ, None),
            P("s", None, SEQ, None),
            P("s", None, SEQ, None),
            P(SEQ, None),
            P(SEQ, None),
            P(ALL, None, None),
            P(None, "s", None),
            P(),
            P(),
            P(),
        ),
        out_specs=(P(ALL, None, None), P(None, ALL)),
        check_vma=False,
    )
```

```python
import math

import jax
import jax.numpy as jnp
import numpy as np
from jax import lax
from jax.experimental import pallas as pl
from jax.experimental.pallas import tpu as pltpu
from jax.sharding import Mesh, PartitionSpec as P

HEADS = 16
HEAD_DIM = 72


CONTRACT_LAST = (((1,), (1,)), ((), ()))


CONTRACT_FIRST = (((0,), (0,)), ((), ()))
SCALE = 1.0 / math.sqrt(HEAD_DIM)
CAP = 300
CAP_PAD = 384


def dot(a, b, dims=(((1,), (0,)), ((), ()))):
    return lax.dot_general(a, b, dims, preferred_element_type=jnp.float32)


def softmax(scores):
    weights = jnp.exp(scores - jnp.max(scores, axis=-1, keepdims=True))
    return weights / jnp.sum(weights, axis=-1, keepdims=True)


def score_grads(attention, prob_grad):
    centred = prob_grad - jnp.sum(prob_grad * attention, axis=-1, keepdims=True)
    return (attention * centred * SCALE).astype(jnp.bfloat16)


def temporal_kernel(grad_ref, query_ref, key_ref, value_ref, out_ref):
    rows, width = grad_ref.shape
    frames = rows // 2
    same = (lax.broadcasted_iota(jnp.int32, (rows, rows), 0) < frames) == (
        lax.broadcasted_iota(jnp.int32, (rows, rows), 1) < frames
    )
    for head in range(HEADS):
        at = slice(head * HEAD_DIM, (head + 1) * HEAD_DIM)
        grad, query, key_rows, value = (
            ref[:, at] for ref in (grad_ref, query_ref, key_ref, value_ref)
        )
        scores = jnp.where(same, dot(query, key_rows, CONTRACT_LAST) * SCALE, -jnp.inf)
        attention = softmax(scores)
        score_grad = score_grads(attention, dot(grad, value, CONTRACT_LAST))
        for part, result in enumerate(
            (
                dot(score_grad, key_rows),
                dot(score_grad, query, CONTRACT_FIRST),
                dot(attention.astype(jnp.bfloat16), grad, CONTRACT_FIRST),
            )
        ):
            start = part * width + head * HEAD_DIM
            out_ref[:, start : start + HEAD_DIM] = result.astype(jnp.bfloat16)


def temporal_grads(grad_heads, query, key_rows, value):
    rows, width = grad_heads.shape
    return pl.pallas_call(
        temporal_kernel,
        out_shape=jax.ShapeDtypeStruct((rows, 3 * width), jnp.bfloat16),
        compiler_params=pltpu.CompilerParams(vmem_limit_bytes=24 << 20),
        cost_estimate=pl.CostEstimate(
            flops=rows * width, bytes_accessed=2 * rows * width, transcendentals=0
        ),
        name="temporal_grads",
    )(grad_heads, query, key_rows, value)


def mixed_kernel(
    place_ref, mine_ref, other_ref, residual_ref, w0, w1, w2, w3, out_ref, held, rows_ref, added, sems
):
    copies = [
        pltpu.make_async_copy(block, held.at[place_ref[i]], sems.at[i])
        for i, block in enumerate((w0, w1, w2, w3))
    ]
    copies.append(pltpu.make_async_copy(residual_ref, added, sems.at[4]))
    for copy in copies:
        copy.start()
    rows_ref[place_ref[4]] = mine_ref[...]
    rows_ref[1 - place_ref[4]] = other_ref[...]
    for copy in copies:
        copy.wait()
    depth = held.shape[2]
    product = dot(
        rows_ref[...].reshape(-1, depth), held[...].reshape(-1, depth), CONTRACT_LAST
    )
    out_ref[...] = (added[...] + product).astype(jnp.bfloat16)


def mixed_half(places, mine, other, residual, blocks):
    in_vmem = pl.BlockSpec(memory_space=pltpu.VMEM)
    rows, depth = mine.shape
    return pl.pallas_call(
        mixed_kernel,
        in_specs=[pl.BlockSpec(memory_space=pltpu.SMEM), in_vmem, in_vmem]
        + [pl.BlockSpec(memory_space=pl.ANY)] * 5,
        out_specs=in_vmem,
        out_shape=jax.ShapeDtypeStruct(residual.shape, jnp.bfloat16),
        scratch_shapes=[
            pltpu.VMEM((4,) + blocks[0].shape, jnp.bfloat16),
            pltpu.VMEM((2, rows, depth), jnp.bfloat16),
            pltpu.VMEM(residual.shape, jnp.float32),
            pltpu.SemaphoreType.DMA((5,)),
        ],
        compiler_params=pltpu.CompilerParams(vmem_limit_bytes=24 << 20),
        cost_estimate=pl.CostEstimate(
            flops=2 * residual.size * depth, bytes_accessed=8 << 20, transcendentals=0
        ),
        name="mixed_half",
    )(places, mine, other, residual, *blocks)


def probs_kernel(length_ref, query_ref, key_ref, probs_ref):
    rows = query_ref.shape[0]
    valid = lax.broadcasted_iota(jnp.int32, (rows, CAP_PAD), 1) < length_ref[0]
    for head in range(HEADS):
        at = slice(head * HEAD_DIM, (head + 1) * HEAD_DIM)
        scores = dot(query_ref[:, at], key_ref[:, at], CONTRACT_LAST) * SCALE
        probs_ref[head] = softmax(jnp.where(valid, scores, -1e30))


def cross_probs(cap_length, cross_query, cap_key):
    rows, width = cross_query.shape
    in_vmem = pl.BlockSpec(memory_space=pltpu.VMEM)
    return pl.pallas_call(
        probs_kernel,
        in_specs=[pl.BlockSpec(memory_space=pltpu.SMEM), in_vmem, in_vmem],
        out_specs=in_vmem,
        out_shape=jax.ShapeDtypeStruct((HEADS, rows, CAP_PAD), jnp.float32),
        compiler_params=pltpu.CompilerParams(vmem_limit_bytes=16 << 20),
        cost_estimate=pl.CostEstimate(
            flops=2 * rows * CAP_PAD * width,
            bytes_accessed=4 << 20,
            transcendentals=HEADS * rows * CAP_PAD,
        ),
        name="cross_probs",
    )(cap_length, cross_query, cap_key)


def cross_kernel(
    arrived_hbm,
    w_out_hbm,
    query_hbm,
    key_hbm,
    value_hbm,
    probs_ref,
    cq_ref,
    terms_ref,
    arrived_ref,
    w_out_ref,
    query_ref,
    key_ref,
    value_ref,
    og_ref,
    sems,
):
    held = (arrived_ref, w_out_ref, query_ref, key_ref, value_ref)
    copies = [
        pltpu.make_async_copy(source, target, sems.at[i])
        for i, (source, target) in enumerate(
            zip((arrived_hbm, w_out_hbm, query_hbm, key_hbm, value_hbm), held)
        )
    ]
    for copy in copies:
        copy.start()
    for copy in copies[:2]:
        copy.wait()
    og_ref[...] = dot(arrived_ref[...], w_out_ref[...]).astype(jnp.bfloat16)
    for copy in copies[2:]:
        copy.wait()
    rest = jnp.zeros((HEAD_DIM, 640 - CAP_PAD), jnp.float32)
    for head in range(HEADS):
        at = slice(head * HEAD_DIM, (head + 1) * HEAD_DIM)
        query, out_grad, key_rows, value = (
            ref[:, at] for ref in (query_ref, og_ref, key_ref, value_ref)
        )
        attention = probs_ref[head]
        score_grad = score_grads(attention, dot(out_grad, value, CONTRACT_LAST))
        cq_ref[:, at] = dot(score_grad, key_rows).astype(jnp.bfloat16)
        key_term = dot(query, score_grad, CONTRACT_FIRST)
        value_term = dot(out_grad, attention.astype(jnp.bfloat16), CONTRACT_FIRST)
        shifted = pltpu.roll(jnp.concatenate([value_term, rest], axis=1), CAP, 1)
        terms_ref[head] = (jnp.concatenate([key_term, rest], axis=1) + shifted).astype(
            jnp.bfloat16
        )


def cross_grads(arrived, w_out, cross_query, cap_key, cap_value, probs):
    rows, width = cross_query.shape
    in_vmem = pl.BlockSpec(memory_space=pltpu.VMEM)
    copied = (arrived, w_out, cross_query, cap_key, cap_value)
    return pl.pallas_call(
        cross_kernel,
        in_specs=[pl.BlockSpec(memory_space=pl.ANY)] * 5 + [in_vmem],
        out_specs=(in_vmem,) * 2,
        out_shape=(
            jax.ShapeDtypeStruct((rows, width), jnp.bfloat16),
            jax.ShapeDtypeStruct((HEADS, HEAD_DIM, 640), jnp.bfloat16),
        ),
        scratch_shapes=[pltpu.VMEM(array.shape, array.dtype) for array in copied]
        + [pltpu.VMEM((rows, width), jnp.bfloat16), pltpu.SemaphoreType.DMA((5,))],
        compiler_params=pltpu.CompilerParams(vmem_limit_bytes=24 << 20),
        cost_estimate=pl.CostEstimate(
            flops=8 * rows * CAP_PAD * width + 2 * rows * width * arrived.shape[1],
            bytes_accessed=12 << 20,
            transcendentals=0,
        ),
        name="cross_grads",
    )(*copied, probs)


ALL = ("s", "x", "y", "z", "c")
SEQ = ("x", "y", "z", "c")
SHAPE = (2, 4, 4, 4, 2)


def flat(s, x, y, z, c):
    return (((s * 4 + x) * 4 + y) * 4 + z) * 2 + c


def ring_groups(first):
    groups = []
    for s in range(2):
        for z in range(4):
            for fixed in range(4):
                groups.append([flat(s, i, fixed, z, first) for i in range(4)])
                groups.append([flat(s, fixed, i, z, 1 - first) for i in range(4)])
    return groups


def gather_groups(block, groups):
    copies = jnp.broadcast_to(block[None], (4,) + block.shape)
    return lax.all_to_all(copies, ALL, 0, 0, axis_index_groups=groups)


def shift_last(block, step):
    pairs = []
    for s in range(2):
        for x in range(4):
            for y in range(4):
                for z in range(4):
                    pairs.append((flat(s, x, y, z, 0), flat(s, x, (y + step) % 4, z, 0)))
                    pairs.append((flat(s, x, y, z, 1), flat(s, (x + step) % 4, y, z, 1)))
    return lax.ppermute(block, ALL, pairs)


def swap_cores(block):
    return lax.ppermute(block, "c", [(0, 1), (1, 0)])


def in_core_order(mine, other):
    core = lax.axis_index("c")
    return jnp.stack([jnp.where(core == 0, mine, other), jnp.where(core == 0, other, mine)])


def feature_order():
    order = np.full((2, 4, 4, 40), -1, np.int32)
    for c in range(2):
        for i in range(4):
            for j in range(4):
                x, y = (j, i) if c == 0 else (i, j)
                for q in range(36):
                    order[c, i, j, q] = 72 * (4 * x + y) + 18 * (q // 9) + 9 * c + q % 9
    return order.reshape(1280)


def cross_halves(cross_weights):
    core = lax.axis_index("c")
    side = lax.axis_index("s")

    def place(z):
        return (z % 2, z // 2)

    pairs = []
    for x in range(4):
        for y in range(4):
            for z in range(8):
                for c in range(2):
                    to = (z + (1 if c == 0 else 7)) % 8
                    s0, z0 = place(z)
                    s1, z1 = place(to)
                    pairs.append((flat(s0, x, y, z0, c), flat(s1, x, y, z1, c)))
    part = lax.dynamic_index_in_dim(cross_weights, core, 0, keepdims=False)
    got = lax.ppermute(part, ALL, pairs)
    swapped = lax.ppermute(got, "c", [(0, 1), (1, 0)])
    other = jnp.stack([jnp.where(core == 0, got, swapped), jnp.where(core == 0, swapped, got)])
    low = jnp.where(side == 0, cross_weights, other)
    high = jnp.where(side == 0, other, cross_weights)
    return jnp.concatenate([low, high], axis=1)


def local(
    grad_out,
    t_query,
    t_key,
    t_value,
    t_out_weight,
    t_qkv_weight,
    frame_input,
    cross_weights,
    cap_key,
    cap_value,
    cap_length,
):
    width = grad_out.shape[-1]
    core = lax.axis_index("c")
    grad_rows = grad_out.reshape(-1, width)
    rows = grad_rows.shape[0]
    place = (jnp.asarray(feature_order())[:, None] == jnp.arange(width)[None, :]).astype(
        jnp.bfloat16
    )
    place_mine = lax.dynamic_slice(place, (core * 640, 0), (640, width))
    grad_both = in_core_order(grad_rows, swap_cores(grad_rows)).reshape(2 * rows, width)
    shard = jnp.concatenate([t_out_weight, t_qkv_weight], axis=1).reshape(2, -1)
    column = lax.all_to_all(jnp.broadcast_to(shard[None], (4,) + shard.shape), "z", 0, 0)
    column = jnp.pad(column.reshape(36, 4 * width), ((0, 4), (0, 0)))
    near = gather_groups(column, ring_groups(0))
    residual = lax.dot_general(
        grad_both, place_mine, CONTRACT_LAST, preferred_element_type=jnp.float32
    )
    padding = ((0, CAP_PAD - CAP), (0, 0))
    cap_key, cap_value = jnp.pad(cap_key, padding), jnp.pad(cap_value, padding)
    near, cross_weights, grad_both, residual, place, cap_key, cap_value = (
        lax.optimization_barrier(
            (near, cross_weights, grad_both, residual, place, cap_key, cap_value)
        )
    )
    qkv_near = near[:, :, width:].reshape(160, 3 * width)
    blocks = [qkv_near] + [shift_last(qkv_near, step) for step in (1, 3, 2)]
    place_here = jnp.where(core == 0, lax.axis_index("y"), lax.axis_index("x"))
    slots = (place_here - jnp.array([0, 1, 3, 2], jnp.int32)) % 4
    places = jnp.concatenate([slots, core.reshape(1)])
    out_mine = gather_groups(near[:, :, :width], ring_groups(1)).reshape(640, width)
    full_cross = cross_halves(cross_weights)
    heads_mine = (
        lax.dot_general(grad_both, out_mine, CONTRACT_LAST, preferred_element_type=jnp.float32)
        .astype(jnp.bfloat16)
        .reshape(2, rows, 640)
    )
    kept = lax.dynamic_index_in_dim(heads_mine, core, 0, keepdims=False)
    sent = lax.dynamic_index_in_dim(heads_mine, 1 - core, 0, keepdims=False)
    heads_parts = in_core_order(kept, swap_cores(sent))
    grad_heads = jnp.dot(
        jnp.concatenate([heads_parts[0], heads_parts[1]], axis=1),
        place,
        preferred_element_type=jnp.float32,
    ).astype(jnp.bfloat16)
    qkv_grad = temporal_grads(
        grad_heads, *(saved.reshape(rows, width) for saved in (t_query, t_key, t_value))
    )
    qkv_grad, *blocks = lax.optimization_barrier((qkv_grad, *blocks))
    mixed = mixed_half(
        places, qkv_grad, swap_cores(qkv_grad), residual, blocks
    ).reshape(2, rows, 640)
    w_out_placed = lax.dot_general(
        place, full_cross[1], CONTRACT_LAST, preferred_element_type=jnp.float32
    ).astype(jnp.bfloat16)
    cross_query = jnp.dot(
        frame_input.reshape(rows, width), full_cross[0], preferred_element_type=jnp.float32
    ).astype(jnp.bfloat16)
    probs = cross_probs(cap_length, cross_query, cap_key)
    arrived = lax.all_to_all(mixed.transpose(1, 0, 2), SEQ, split_axis=0, concat_axis=0)
    arrived = arrived.reshape(64, 2, 2, 640).transpose(0, 2, 1, 3).reshape(128, 1280)
    cq_grad, terms = cross_grads(arrived, w_out_placed, cross_query, cap_key, cap_value, probs)
    grad_input = (
        jnp.dot(arrived, place, preferred_element_type=jnp.float32)
        + lax.dot_general(cq_grad, full_cross[0], CONTRACT_LAST, preferred_element_type=jnp.float32)
    ).astype(jnp.bfloat16)
    head = jnp.sum(lax.all_to_all(terms, ("x", "y"), 0, 0).astype(jnp.float32), axis=0)
    head = head.astype(jnp.bfloat16)
    pieces = jnp.concatenate(
        [head[:, :CAP].reshape(8, 9, CAP), head[:, CAP : 2 * CAP].reshape(8, 9, CAP)]
    )
    piece = jnp.sum(lax.all_to_all(pieces, ("s", "z", "c"), 0, 0).astype(jnp.float32), axis=0)
    return (grad_input.reshape(frame_input.shape), piece.T)


def solution(mesh):
    fine = Mesh(mesh.devices.reshape(SHAPE), ALL)
    return jax.shard_map(
        local,
        mesh=fine,
        in_specs=(
            P("s", None, SEQ, None),
            P("s", None, SEQ, None),
            P("s", None, SEQ, None),
            P("s", None, SEQ, None),
            P(SEQ, None),
            P(SEQ, None),
            P(ALL, None, None),
            P(None, "s", None),
            P(),
            P(),
            P(),
        ),
        out_specs=(P(ALL, None, None), P(None, ALL)),
        check_vma=False,
    )
```

```python
import math

import jax
import jax.numpy as jnp
import numpy as np
from jax import lax
from jax.experimental import pallas as pl
from jax.experimental.pallas import tpu as pltpu
from jax.sharding import Mesh, PartitionSpec as P

HEADS = 16
HEAD_DIM = 72


CONTRACT_LAST = (((1,), (1,)), ((), ()))


CONTRACT_FIRST = (((0,), (0,)), ((), ()))
SCALE = 1.0 / math.sqrt(HEAD_DIM)
CAP = 300
CAP_PAD = 384


def dot(a, b, dims=(((1,), (0,)), ((), ()))):
    return lax.dot_general(a, b, dims, preferred_element_type=jnp.float32)


def softmax(scores):
    weights = jnp.exp(scores - jnp.max(scores, axis=-1, keepdims=True))
    return weights / jnp.sum(weights, axis=-1, keepdims=True)


def score_grads(attention, prob_grad):
    centred = prob_grad - jnp.sum(prob_grad * attention, axis=-1, keepdims=True)
    return (attention * centred * SCALE).astype(jnp.bfloat16)


def temporal_kernel(grad_ref, query_ref, key_ref, value_ref, out_ref):
    rows, width = grad_ref.shape
    frames = rows // 2
    same = (lax.broadcasted_iota(jnp.int32, (rows, rows), 0) < frames) == (
        lax.broadcasted_iota(jnp.int32, (rows, rows), 1) < frames
    )
    for head in range(HEADS):
        at = slice(head * HEAD_DIM, (head + 1) * HEAD_DIM)
        grad, query, key_rows, value = (
            ref[:, at] for ref in (grad_ref, query_ref, key_ref, value_ref)
        )
        scores = jnp.where(same, dot(query, key_rows, CONTRACT_LAST) * SCALE, -jnp.inf)
        attention = softmax(scores)
        score_grad = score_grads(attention, dot(grad, value, CONTRACT_LAST))
        for part, result in enumerate(
            (
                dot(score_grad, key_rows),
                dot(score_grad, query, CONTRACT_FIRST),
                dot(attention.astype(jnp.bfloat16), grad, CONTRACT_FIRST),
            )
        ):
            start = part * width + head * HEAD_DIM
            out_ref[:, start : start + HEAD_DIM] = result.astype(jnp.bfloat16)


def temporal_grads(grad_heads, query, key_rows, value):
    rows, width = grad_heads.shape
    return pl.pallas_call(
        temporal_kernel,
        out_shape=jax.ShapeDtypeStruct((rows, 3 * width), jnp.bfloat16),
        compiler_params=pltpu.CompilerParams(vmem_limit_bytes=24 << 20),
        cost_estimate=pl.CostEstimate(
            flops=rows * width, bytes_accessed=2 * rows * width, transcendentals=0
        ),
        name="temporal_grads",
    )(grad_heads, query, key_rows, value)


def mixed_kernel(
    place_ref, mine_ref, other_ref, residual_ref, w0, w1, w2, w3, out_ref, held, rows_ref, added, sems
):
    copies = [
        pltpu.make_async_copy(block, held.at[place_ref[i]], sems.at[i])
        for i, block in enumerate((w0, w1, w2, w3))
    ]
    copies.append(pltpu.make_async_copy(residual_ref, added, sems.at[4]))
    for copy in copies:
        copy.start()
    rows_ref[place_ref[4]] = mine_ref[...]
    rows_ref[1 - place_ref[4]] = other_ref[...]
    for copy in copies:
        copy.wait()
    depth = held.shape[2]
    product = dot(
        rows_ref[...].reshape(-1, depth), held[...].reshape(-1, depth), CONTRACT_LAST
    )
    made = product.shape[1]
    out_ref[:, :made] = (added[:, :made].astype(jnp.float32) + product).astype(jnp.bfloat16)
    out_ref[:, made:] = jnp.zeros((out_ref.shape[0], out_ref.shape[1] - made), jnp.bfloat16)


def mixed_half(places, mine, other, residual, blocks):
    in_vmem = pl.BlockSpec(memory_space=pltpu.VMEM)
    rows, depth = mine.shape
    return pl.pallas_call(
        mixed_kernel,
        in_specs=[pl.BlockSpec(memory_space=pltpu.SMEM), in_vmem, in_vmem]
        + [pl.BlockSpec(memory_space=pl.ANY)] * 5,
        out_specs=in_vmem,
        out_shape=jax.ShapeDtypeStruct(residual.shape, jnp.bfloat16),
        scratch_shapes=[
            pltpu.VMEM((4,) + blocks[0].shape, jnp.bfloat16),
            pltpu.VMEM((2, rows, depth), jnp.bfloat16),
            pltpu.VMEM(residual.shape, jnp.bfloat16),
            pltpu.SemaphoreType.DMA((5,)),
        ],
        compiler_params=pltpu.CompilerParams(vmem_limit_bytes=24 << 20),
        cost_estimate=pl.CostEstimate(
            flops=2 * residual.size * depth, bytes_accessed=8 << 20, transcendentals=0
        ),
        name="mixed_half",
    )(places, mine, other, residual, *blocks)


def probs_kernel(length_ref, query_ref, key_ref, probs_ref):
    rows = query_ref.shape[0]
    valid = lax.broadcasted_iota(jnp.int32, (rows, CAP_PAD), 1) < length_ref[0]
    for head in range(HEADS):
        at = slice(head * HEAD_DIM, (head + 1) * HEAD_DIM)
        scores = dot(query_ref[:, at], key_ref[:, at], CONTRACT_LAST) * SCALE
        probs_ref[head] = softmax(jnp.where(valid, scores, -1e30))


def cross_probs(cap_length, cross_query, cap_key):
    rows, width = cross_query.shape
    in_vmem = pl.BlockSpec(memory_space=pltpu.VMEM)
    return pl.pallas_call(
        probs_kernel,
        in_specs=[pl.BlockSpec(memory_space=pltpu.SMEM), in_vmem, in_vmem],
        out_specs=in_vmem,
        out_shape=jax.ShapeDtypeStruct((HEADS, rows, CAP_PAD), jnp.float32),
        compiler_params=pltpu.CompilerParams(vmem_limit_bytes=16 << 20),
        cost_estimate=pl.CostEstimate(
            flops=2 * rows * CAP_PAD * width,
            bytes_accessed=4 << 20,
            transcendentals=HEADS * rows * CAP_PAD,
        ),
        name="cross_probs",
    )(cap_length, cross_query, cap_key)


def cross_kernel(
    core_ref,
    arrived_hbm,
    w_out_hbm,
    query_hbm,
    value_hbm,
    probs_hbm,
    key_hbm,
    cq_ref,
    keep_ref,
    send_ref,
    arrived_ref,
    w_out_ref,
    query_ref,
    value_ref,
    probs_ref,
    key_ref,
    og_ref,
    sems,
):
    held = (arrived_ref, w_out_ref, query_ref, value_ref, probs_ref, key_ref)
    given = (arrived_hbm, w_out_hbm, query_hbm, value_hbm, probs_hbm, key_hbm)
    copies = [
        pltpu.make_async_copy(source, target, sems.at[i])
        for i, (source, target) in enumerate(zip(given, held))
    ]
    for copy in copies:
        copy.start()
    for copy in copies[:2]:
        copy.wait()
    og_ref[...] = dot(arrived_ref[...], w_out_ref[...]).astype(jnp.bfloat16)
    for copy in copies[2:]:
        copy.wait()
    first = core_ref[0] == 0
    for head in range(HEADS):
        at = slice(head * HEAD_DIM, (head + 1) * HEAD_DIM)
        query, out_grad, key_rows, value = (
            ref[:, at] for ref in (query_ref, og_ref, key_ref, value_ref)
        )
        attention = probs_ref[head]
        score_grad = score_grads(attention, dot(out_grad, value, CONTRACT_LAST))
        cq_ref[:, at] = dot(score_grad, key_rows).astype(jnp.bfloat16)
        key_term = dot(query, score_grad, CONTRACT_FIRST)
        value_term = dot(out_grad, attention.astype(jnp.bfloat16), CONTRACT_FIRST)
        keep_ref[head] = jnp.where(first, key_term, value_term).astype(jnp.bfloat16)
        send_ref[head] = jnp.where(first, value_term, key_term).astype(jnp.bfloat16)


def cross_grads(core, arrived, w_out, cross_query, cap_value, probs, cap_key):
    rows, width = cross_query.shape
    in_vmem = pl.BlockSpec(memory_space=pltpu.VMEM)
    copied = (arrived, w_out, cross_query, cap_value, probs, cap_key)
    term = jax.ShapeDtypeStruct((HEADS, HEAD_DIM, CAP_PAD), jnp.bfloat16)
    return pl.pallas_call(
        cross_kernel,
        in_specs=[pl.BlockSpec(memory_space=pltpu.SMEM)]
        + [pl.BlockSpec(memory_space=pl.ANY)] * 6,
        out_specs=(in_vmem,) * 3,
        out_shape=(jax.ShapeDtypeStruct((rows, width), jnp.bfloat16), term, term),
        scratch_shapes=[pltpu.VMEM(array.shape, array.dtype) for array in copied]
        + [pltpu.VMEM((rows, width), jnp.bfloat16), pltpu.SemaphoreType.DMA((6,))],
        compiler_params=pltpu.CompilerParams(vmem_limit_bytes=56 << 20),
        cost_estimate=pl.CostEstimate(
            flops=8 * rows * CAP_PAD * width + 2 * rows * width * arrived.shape[1],
            bytes_accessed=12 << 20,
            transcendentals=0,
        ),
        name="cross_grads",
    )(core, *copied)


ALL = ("s", "x", "y", "z", "c")
SEQ = ("x", "y", "z", "c")
SHAPE = (2, 4, 4, 4, 2)


def flat(s, x, y, z, c):
    return (((s * 4 + x) * 4 + y) * 4 + z) * 2 + c


def ring_groups(first):
    groups = []
    for s in range(2):
        for z in range(4):
            for fixed in range(4):
                groups.append([flat(s, i, fixed, z, first) for i in range(4)])
                groups.append([flat(s, fixed, i, z, 1 - first) for i in range(4)])
    return groups


def gather_groups(block, groups):
    copies = jnp.broadcast_to(block[None], (4,) + block.shape)
    return lax.all_to_all(copies, ALL, 0, 0, axis_index_groups=groups)


def shift_last(block, step):
    pairs = []
    for s in range(2):
        for x in range(4):
            for y in range(4):
                for z in range(4):
                    pairs.append((flat(s, x, y, z, 0), flat(s, x, (y + step) % 4, z, 0)))
                    pairs.append((flat(s, x, y, z, 1), flat(s, (x + step) % 4, y, z, 1)))
    return lax.ppermute(block, ALL, pairs)


def swap_cores(block):
    return lax.ppermute(block, "c", [(0, 1), (1, 0)])


def in_core_order(mine, other):
    core = lax.axis_index("c")
    return jnp.stack([jnp.where(core == 0, mine, other), jnp.where(core == 0, other, mine)])


def feature_order():
    order = np.full((2, 640), -1, np.int32)
    for c in range(2):
        for i in range(4):
            for j in range(4):
                x, y = (j, i) if c == 0 else (i, j)
                for q in range(36):
                    at = (4 * i + j) * 36 + q
                    order[c, at] = 72 * (4 * x + y) + 18 * (q // 9) + 9 * c + q % 9
    return order.reshape(1280)


def cross_halves(cross_weights):
    core = lax.axis_index("c")
    side = lax.axis_index("s")

    def place(z):
        return (z % 2, z // 2)

    pairs = []
    for x in range(4):
        for y in range(4):
            for z in range(8):
                for c in range(2):
                    to = (z + (1 if c == 0 else 7)) % 8
                    s0, z0 = place(z)
                    s1, z1 = place(to)
                    pairs.append((flat(s0, x, y, z0, c), flat(s1, x, y, z1, c)))
    part = lax.dynamic_index_in_dim(cross_weights, core, 0, keepdims=False)
    got = lax.ppermute(part, ALL, pairs)
    swapped = lax.ppermute(got, "c", [(0, 1), (1, 0)])
    other = jnp.stack([jnp.where(core == 0, got, swapped), jnp.where(core == 0, swapped, got)])
    low = jnp.where(side == 0, cross_weights, other)
    high = jnp.where(side == 0, other, cross_weights)
    return jnp.concatenate([low, high], axis=1)


def local(
    grad_out,
    t_query,
    t_key,
    t_value,
    t_out_weight,
    t_qkv_weight,
    frame_input,
    cross_weights,
    cap_key,
    cap_value,
    cap_length,
):
    width = grad_out.shape[-1]
    core = lax.axis_index("c")
    grad_rows = grad_out.reshape(-1, width)
    rows = grad_rows.shape[0]
    place = (jnp.asarray(feature_order())[:, None] == jnp.arange(width)[None, :]).astype(
        jnp.bfloat16
    )
    place_mine = lax.dynamic_slice(place, (core * 640, 0), (640, width))
    grad_both = in_core_order(grad_rows, swap_cores(grad_rows)).reshape(2 * rows, width)
    shard = jnp.concatenate([t_out_weight, t_qkv_weight], axis=1).reshape(2, -1)
    column = lax.all_to_all(jnp.broadcast_to(shard[None], (4,) + shard.shape), "z", 0, 0)
    column = jnp.pad(column.reshape(36, 4 * width), ((0, 4), (0, 0)))
    near = gather_groups(column, ring_groups(0))
    residual = lax.dot_general(
        grad_both, place_mine, CONTRACT_LAST, preferred_element_type=jnp.float32
    ).astype(jnp.bfloat16)
    padding = ((0, CAP_PAD - CAP), (0, 0))
    cap_key, cap_value = jnp.pad(cap_key, padding), jnp.pad(cap_value, padding)
    out_near = near[:, :36, :width].reshape(144, width)
    out_near, cross_weights, grad_both, residual, place, cap_key, cap_value = (
        lax.optimization_barrier(
            (out_near, cross_weights, grad_both, residual, place, cap_key, cap_value)
        )
    )
    qkv_near = near[:, :36, width:].reshape(144, 3 * width)
    blocks = [qkv_near] + [shift_last(qkv_near, step) for step in (1, 3, 2)]
    place_here = jnp.where(core == 0, lax.axis_index("y"), lax.axis_index("x"))
    slots = (place_here - jnp.array([0, 1, 3, 2], jnp.int32)) % 4
    places = jnp.concatenate([slots, core.reshape(1)])
    out_mine = gather_groups(out_near, ring_groups(1)).reshape(576, width)
    full_cross = cross_halves(cross_weights)
    heads_mine = (
        lax.dot_general(grad_both, out_mine, CONTRACT_LAST, preferred_element_type=jnp.float32)
        .astype(jnp.bfloat16)
        .reshape(2, rows, 576)
    )
    kept = lax.dynamic_index_in_dim(heads_mine, core, 0, keepdims=False)
    sent = lax.dynamic_index_in_dim(heads_mine, 1 - core, 0, keepdims=False)
    heads_parts = in_core_order(kept, swap_cores(sent))
    grad_heads = (
        jnp.dot(heads_parts[0], place[:576], preferred_element_type=jnp.float32)
        + jnp.dot(heads_parts[1], place[640:1216], preferred_element_type=jnp.float32)
    ).astype(jnp.bfloat16)
    qkv_grad = temporal_grads(
        grad_heads, *(saved.reshape(rows, width) for saved in (t_query, t_key, t_value))
    )
    qkv_grad, *blocks = lax.optimization_barrier((qkv_grad, *blocks))
    mixed = mixed_half(
        places, qkv_grad, swap_cores(qkv_grad), residual, blocks
    ).reshape(2, rows, 640)
    w_out_placed = lax.dot_general(
        place, full_cross[1], CONTRACT_LAST, preferred_element_type=jnp.float32
    ).astype(jnp.bfloat16)
    cross_query = jnp.dot(
        frame_input.reshape(rows, width), full_cross[0], preferred_element_type=jnp.float32
    ).astype(jnp.bfloat16)
    probs = cross_probs(cap_length, cross_query, cap_key)
    arrived = lax.all_to_all(mixed.transpose(1, 0, 2), SEQ, split_axis=0, concat_axis=0)
    arrived = arrived.reshape(64, 2, 2, 640).transpose(0, 2, 1, 3).reshape(128, 1280)
    cq_grad, keep, send = cross_grads(
        core.reshape(1), arrived, w_out_placed, cross_query, cap_value, probs, cap_key
    )
    chip = (keep.astype(jnp.float32) + swap_cores(send).astype(jnp.float32)).astype(jnp.bfloat16)
    grad_input = (
        jnp.dot(arrived, place, preferred_element_type=jnp.float32)
        + lax.dot_general(cq_grad, full_cross[0], CONTRACT_LAST, preferred_element_type=jnp.float32)
    ).astype(jnp.bfloat16)
    head = jnp.sum(lax.all_to_all(chip, ("x", "y"), 0, 0).astype(jnp.float32), axis=0)
    pieces = head[:, :CAP].astype(jnp.bfloat16).reshape(1, 8, 9, CAP)
    sides = jnp.arange(2).reshape(2, 1, 1, 1) == core
    pieces = jnp.where(sides, pieces, jnp.zeros_like(pieces)).reshape(16, 9, CAP)
    piece = jnp.sum(lax.all_to_all(pieces, ("s", "z", "c"), 0, 0).astype(jnp.float32), axis=0)
    return (grad_input.reshape(frame_input.shape), piece.T)


def solution(mesh):
    fine = Mesh(mesh.devices.reshape(SHAPE), ALL)
    return jax.shard_map(
        local,
        mesh=fine,
        in_specs=(
            P("s", None, SEQ, None),
            P("s", None, SEQ, None),
            P("s", None, SEQ, None),
            P("s", None, SEQ, None),
            P(SEQ, None),
            P(SEQ, None),
            P(ALL, None, None),
            P(None, "s", None),
            P(),
            P(),
            P(),
        ),
        out_specs=(P(ALL, None, None), P(None, ALL)),
        check_vma=False,
    )
```

```python
import math

import jax
import jax.numpy as jnp
import numpy as np
from jax import lax
from jax.experimental import pallas as pl
from jax.experimental.pallas import tpu as pltpu
from jax.sharding import Mesh, PartitionSpec as P

HEADS = 16
HEAD_DIM = 72


CONTRACT_LAST = (((1,), (1,)), ((), ()))


CONTRACT_FIRST = (((0,), (0,)), ((), ()))
SCALE = 1.0 / math.sqrt(HEAD_DIM)
CAP = 300
CAP_PAD = 384


def dot(a, b, dims=(((1,), (0,)), ((), ()))):
    return lax.dot_general(a, b, dims, preferred_element_type=jnp.float32)


def softmax(scores):
    weights = jnp.exp(scores - jnp.max(scores, axis=-1, keepdims=True))
    return weights / jnp.sum(weights, axis=-1, keepdims=True)


def score_grads(attention, prob_grad):
    centred = prob_grad - jnp.sum(prob_grad * attention, axis=-1, keepdims=True)
    return (attention * centred * SCALE).astype(jnp.bfloat16)


def temporal_kernel(
    core_ref, kept_ref, got_ref, order_ref, query_ref, key_ref, value_ref, out_ref, grad_ref
):
    rows, width = query_ref.shape
    half = kept_ref.shape[1]
    start = order_ref.shape[0] // 2
    kept, got = kept_ref[...], got_ref[...]
    first = core_ref[0] == 0
    grad_ref[...] = (
        dot(jnp.where(first, kept, got), order_ref[:half])
        + dot(jnp.where(first, got, kept), order_ref[start : start + half])
    ).astype(jnp.bfloat16)
    frames = rows // 2
    same = (lax.broadcasted_iota(jnp.int32, (rows, rows), 0) < frames) == (
        lax.broadcasted_iota(jnp.int32, (rows, rows), 1) < frames
    )
    for head in range(HEADS):
        at = slice(head * HEAD_DIM, (head + 1) * HEAD_DIM)
        grad, query, key_rows, value = (
            ref[:, at] for ref in (grad_ref, query_ref, key_ref, value_ref)
        )
        scores = jnp.where(same, dot(query, key_rows, CONTRACT_LAST) * SCALE, -jnp.inf)
        attention = softmax(scores)
        score_grad = score_grads(attention, dot(grad, value, CONTRACT_LAST))
        for part, result in enumerate(
            (
                dot(score_grad, key_rows),
                dot(score_grad, query, CONTRACT_FIRST),
                dot(attention.astype(jnp.bfloat16), grad, CONTRACT_FIRST),
            )
        ):
            start = part * width + head * HEAD_DIM
            out_ref[:, start : start + HEAD_DIM] = result.astype(jnp.bfloat16)


def temporal_grads(core, kept, got, order, query, key_rows, value):
    rows, width = query.shape
    return pl.pallas_call(
        temporal_kernel,
        in_specs=[pl.BlockSpec(memory_space=pltpu.SMEM)]
        + [pl.BlockSpec(memory_space=pltpu.VMEM)] * 6,
        out_specs=pl.BlockSpec(memory_space=pltpu.VMEM),
        out_shape=jax.ShapeDtypeStruct((rows, 3 * width), jnp.bfloat16),
        scratch_shapes=[pltpu.VMEM((rows, width), jnp.bfloat16)],
        compiler_params=pltpu.CompilerParams(vmem_limit_bytes=16 << 20),
        cost_estimate=pl.CostEstimate(
            flops=rows * width, bytes_accessed=2 * rows * width, transcendentals=0
        ),
        name="temporal_grads",
    )(core, kept, got, order, query, key_rows, value)


def mixed_kernel(
    place_ref, mine_ref, other_ref, residual_ref, w0, w1, w2, w3, out_ref, held, rows_ref, added, sems
):
    copies = [
        pltpu.make_async_copy(block, held.at[place_ref[i]], sems.at[i])
        for i, block in enumerate((w0, w1, w2, w3))
    ]
    copies.append(pltpu.make_async_copy(residual_ref, added, sems.at[4]))
    for copy in copies:
        copy.start()
    rows_ref[place_ref[4]] = mine_ref[...]
    rows_ref[1 - place_ref[4]] = other_ref[...]
    for copy in copies:
        copy.wait()
    depth = held.shape[2]
    product = dot(
        rows_ref[...].reshape(-1, depth), held[...].reshape(-1, depth), CONTRACT_LAST
    )
    made = product.shape[1]
    out_ref[:, :made] = (added[:, :made].astype(jnp.float32) + product).astype(jnp.bfloat16)
    out_ref[:, made:] = jnp.zeros((out_ref.shape[0], out_ref.shape[1] - made), jnp.bfloat16)


def mixed_half(places, mine, other, residual, blocks):
    in_vmem = pl.BlockSpec(memory_space=pltpu.VMEM)
    rows, depth = mine.shape
    return pl.pallas_call(
        mixed_kernel,
        in_specs=[pl.BlockSpec(memory_space=pltpu.SMEM), in_vmem, in_vmem]
        + [pl.BlockSpec(memory_space=pl.ANY)] * 5,
        out_specs=in_vmem,
        out_shape=jax.ShapeDtypeStruct(residual.shape, jnp.bfloat16),
        scratch_shapes=[
            pltpu.VMEM((4,) + blocks[0].shape, jnp.bfloat16),
            pltpu.VMEM((2, rows, depth), jnp.bfloat16),
            pltpu.VMEM(residual.shape, jnp.bfloat16),
            pltpu.SemaphoreType.DMA((5,)),
        ],
        compiler_params=pltpu.CompilerParams(vmem_limit_bytes=24 << 20),
        cost_estimate=pl.CostEstimate(
            flops=2 * residual.size * depth, bytes_accessed=8 << 20, transcendentals=0
        ),
        name="mixed_half",
    )(places, mine, other, residual, *blocks)


def probs_kernel(length_ref, query_ref, key_ref, probs_ref):
    rows = query_ref.shape[0]
    valid = lax.broadcasted_iota(jnp.int32, (rows, CAP_PAD), 1) < length_ref[0]
    for head in range(HEADS):
        at = slice(head * HEAD_DIM, (head + 1) * HEAD_DIM)
        scores = dot(query_ref[:, at], key_ref[:, at], CONTRACT_LAST) * SCALE
        probs_ref[head] = softmax(jnp.where(valid, scores, -1e30))


def cross_probs(cap_length, cross_query, cap_key):
    rows, width = cross_query.shape
    in_vmem = pl.BlockSpec(memory_space=pltpu.VMEM)
    return pl.pallas_call(
        probs_kernel,
        in_specs=[pl.BlockSpec(memory_space=pltpu.SMEM), in_vmem, in_vmem],
        out_specs=in_vmem,
        out_shape=jax.ShapeDtypeStruct((HEADS, rows, CAP_PAD), jnp.float32),
        compiler_params=pltpu.CompilerParams(vmem_limit_bytes=16 << 20),
        cost_estimate=pl.CostEstimate(
            flops=2 * rows * CAP_PAD * width,
            bytes_accessed=4 << 20,
            transcendentals=HEADS * rows * CAP_PAD,
        ),
        name="cross_probs",
    )(cap_length, cross_query, cap_key)


def cross_kernel(
    core_ref,
    arrived_hbm,
    w_out_hbm,
    query_hbm,
    value_hbm,
    key_hbm,
    probs_ref,
    cq_ref,
    keep_ref,
    send_ref,
    arrived_ref,
    w_out_ref,
    query_ref,
    value_ref,
    key_ref,
    og_ref,
    sems,
):
    held = (arrived_ref, w_out_ref, query_ref, value_ref, key_ref)
    given = (arrived_hbm, w_out_hbm, query_hbm, value_hbm, key_hbm)
    copies = [
        pltpu.make_async_copy(source, target, sems.at[i])
        for i, (source, target) in enumerate(zip(given, held))
    ]
    for copy in copies:
        copy.start()
    for copy in copies[:2]:
        copy.wait()
    og_ref[...] = dot(arrived_ref[...], w_out_ref[...]).astype(jnp.bfloat16)
    for copy in copies[2:]:
        copy.wait()
    first = core_ref[0] == 0
    for head in range(HEADS):
        at = slice(head * HEAD_DIM, (head + 1) * HEAD_DIM)
        query, out_grad, key_rows, value = (
            ref[:, at] for ref in (query_ref, og_ref, key_ref, value_ref)
        )
        attention = probs_ref[head]
        score_grad = score_grads(attention, dot(out_grad, value, CONTRACT_LAST))
        cq_ref[:, at] = dot(score_grad, key_rows).astype(jnp.bfloat16)
        key_term = dot(query, score_grad, CONTRACT_FIRST)
        value_term = dot(out_grad, attention.astype(jnp.bfloat16), CONTRACT_FIRST)
        keep_ref[head] = jnp.where(first, key_term, value_term).astype(jnp.bfloat16)
        send_ref[head] = jnp.where(first, value_term, key_term).astype(jnp.bfloat16)


def cross_grads(core, arrived, w_out, cross_query, cap_value, cap_key, probs):
    rows, width = cross_query.shape
    in_vmem = pl.BlockSpec(memory_space=pltpu.VMEM)
    copied = (arrived, w_out, cross_query, cap_value, cap_key)
    term = jax.ShapeDtypeStruct((HEADS, HEAD_DIM, CAP_PAD), jnp.bfloat16)
    return pl.pallas_call(
        cross_kernel,
        in_specs=[pl.BlockSpec(memory_space=pltpu.SMEM)]
        + [pl.BlockSpec(memory_space=pl.ANY)] * 5
        + [in_vmem],
        out_specs=(in_vmem,) * 3,
        out_shape=(jax.ShapeDtypeStruct((rows, width), jnp.bfloat16), term, term),
        scratch_shapes=[pltpu.VMEM(array.shape, array.dtype) for array in copied]
        + [pltpu.VMEM((rows, width), jnp.bfloat16), pltpu.SemaphoreType.DMA((5,))],
        compiler_params=pltpu.CompilerParams(vmem_limit_bytes=54 << 20),
        cost_estimate=pl.CostEstimate(
            flops=8 * rows * CAP_PAD * width + 2 * rows * width * arrived.shape[1],
            bytes_accessed=12 << 20,
            transcendentals=0,
        ),
        name="cross_grads",
    )(core, *copied, probs)


ALL = ("s", "x", "y", "z", "c")
SEQ = ("x", "y", "z", "c")
SHAPE = (2, 4, 4, 4, 2)


def flat(s, x, y, z, c):
    return (((s * 4 + x) * 4 + y) * 4 + z) * 2 + c


def ring_groups(first):
    groups = []
    for s in range(2):
        for z in range(4):
            for fixed in range(4):
                groups.append([flat(s, i, fixed, z, first) for i in range(4)])
                groups.append([flat(s, fixed, i, z, 1 - first) for i in range(4)])
    return groups


def gather_groups(block, groups):
    copies = jnp.broadcast_to(block[None], (4,) + block.shape)
    return lax.all_to_all(copies, ALL, 0, 0, axis_index_groups=groups)


def shift_last(block, step):
    pairs = []
    for s in range(2):
        for x in range(4):
            for y in range(4):
                for z in range(4):
                    pairs.append((flat(s, x, y, z, 0), flat(s, x, (y + step) % 4, z, 0)))
                    pairs.append((flat(s, x, y, z, 1), flat(s, (x + step) % 4, y, z, 1)))
    return lax.ppermute(block, ALL, pairs)


def swap_cores(block):
    return lax.ppermute(block, "c", [(0, 1), (1, 0)])


def in_core_order(mine, other):
    core = lax.axis_index("c")
    return jnp.stack([jnp.where(core == 0, mine, other), jnp.where(core == 0, other, mine)])


def feature_order():
    order = np.full((2, 640), -1, np.int32)
    for c in range(2):
        for i in range(4):
            for j in range(4):
                x, y = (j, i) if c == 0 else (i, j)
                for q in range(36):
                    at = (4 * i + j) * 36 + q
                    order[c, at] = 72 * (4 * x + y) + 18 * (q // 9) + 9 * c + q % 9
    return order.reshape(1280)


def cross_fetch(part):
    def place(z):
        return (z % 2, z // 2)

    pairs = []
    for x in range(4):
        for y in range(4):
            for z in range(8):
                for c in range(2):
                    to = (z + (1 if c == 0 else 7)) % 8
                    s0, z0 = place(z)
                    s1, z1 = place(to)
                    pairs.append((flat(s0, x, y, z0, c), flat(s1, x, y, z1, c)))
    return lax.ppermute(part, ALL, pairs)


def cross_whole(cross_weights, got):
    core = lax.axis_index("c")
    side = lax.axis_index("s")
    swapped = lax.ppermute(got, "c", [(0, 1), (1, 0)])
    other = jnp.stack([jnp.where(core == 0, got, swapped), jnp.where(core == 0, swapped, got)])
    low = jnp.where(side == 0, cross_weights, other)
    high = jnp.where(side == 0, other, cross_weights)
    return jnp.concatenate([low, high], axis=1)


def local(
    grad_out,
    t_query,
    t_key,
    t_value,
    t_out_weight,
    t_qkv_weight,
    frame_input,
    cross_weights,
    cap_key,
    cap_value,
    cap_length,
):
    width = grad_out.shape[-1]
    core = lax.axis_index("c")
    grad_rows = grad_out.reshape(-1, width)
    rows = grad_rows.shape[0]
    place = (jnp.asarray(feature_order())[:, None] == jnp.arange(width)[None, :]).astype(
        jnp.bfloat16
    )
    place_mine = lax.dynamic_slice(place, (core * 640, 0), (640, width))
    grad_both = in_core_order(grad_rows, swap_cores(grad_rows)).reshape(2 * rows, width)
    shard = jnp.concatenate([t_out_weight, t_qkv_weight], axis=1).reshape(2, -1)
    column = lax.all_to_all(jnp.broadcast_to(shard[None], (4,) + shard.shape), "z", 0, 0)
    column = jnp.pad(column.reshape(36, 4 * width), ((0, 4), (0, 0)))
    near = gather_groups(column, ring_groups(0))
    residual = lax.dot_general(
        grad_both, place_mine, CONTRACT_LAST, preferred_element_type=jnp.float32
    ).astype(jnp.bfloat16)
    padding = ((0, CAP_PAD - CAP), (0, 0))
    cap_key, cap_value = jnp.pad(cap_key, padding), jnp.pad(cap_value, padding)
    out_near = near[:, :36, :width].reshape(144, width)
    cross_part = lax.dynamic_index_in_dim(cross_weights, core, 0, keepdims=False)
    out_near, cross_part, grad_both, residual, place, cap_key, cap_value = (
        lax.optimization_barrier(
            (out_near, cross_part, grad_both, residual, place, cap_key, cap_value)
        )
    )
    qkv_near = near[:, :36, width:].reshape(144, 3 * width)
    blocks = [qkv_near] + [shift_last(qkv_near, step) for step in (1, 3, 2)]
    place_here = jnp.where(core == 0, lax.axis_index("y"), lax.axis_index("x"))
    slots = (place_here - jnp.array([0, 1, 3, 2], jnp.int32)) % 4
    places = jnp.concatenate([slots, core.reshape(1)])
    out_mine = gather_groups(out_near, ring_groups(1)).reshape(576, width)
    cross_part = cross_fetch(cross_part)
    heads_mine = (
        lax.dot_general(grad_both, out_mine, CONTRACT_LAST, preferred_element_type=jnp.float32)
        .astype(jnp.bfloat16)
        .reshape(2, rows, 576)
    )
    kept = lax.dynamic_index_in_dim(heads_mine, core, 0, keepdims=False)
    sent = lax.dynamic_index_in_dim(heads_mine, 1 - core, 0, keepdims=False)
    qkv_grad = temporal_grads(
        core.reshape(1),
        kept,
        swap_cores(sent),
        place,
        *(saved.reshape(rows, width) for saved in (t_query, t_key, t_value)),
    )
    qkv_grad, cross_part, *blocks = lax.optimization_barrier((qkv_grad, cross_part, *blocks))
    full_cross = cross_whole(cross_weights, cross_part)
    mixed = mixed_half(
        places, qkv_grad, swap_cores(qkv_grad), residual, blocks
    ).reshape(2, rows, 640)
    w_out_placed = lax.dot_general(
        place, full_cross[1], CONTRACT_LAST, preferred_element_type=jnp.float32
    ).astype(jnp.bfloat16)
    cross_query = jnp.dot(
        frame_input.reshape(rows, width), full_cross[0], preferred_element_type=jnp.float32
    ).astype(jnp.bfloat16)
    probs = cross_probs(cap_length, cross_query, cap_key)
    arrived = lax.all_to_all(mixed.transpose(1, 0, 2), SEQ, split_axis=0, concat_axis=0)
    arrived = arrived.reshape(64, 2, 2, 640).transpose(0, 2, 1, 3).reshape(128, 1280)
    cq_grad, keep, send = cross_grads(
        core.reshape(1), arrived, w_out_placed, cross_query, cap_value, cap_key, probs
    )
    chip = (keep.astype(jnp.float32) + swap_cores(send).astype(jnp.float32)).astype(jnp.bfloat16)
    grad_input = (
        jnp.dot(arrived, place, preferred_element_type=jnp.float32)
        + lax.dot_general(cq_grad, full_cross[0], CONTRACT_LAST, preferred_element_type=jnp.float32)
    ).astype(jnp.bfloat16)
    head = jnp.sum(lax.all_to_all(chip, ("x", "y"), 0, 0).astype(jnp.float32), axis=0)
    pieces = head[:, :CAP].astype(jnp.bfloat16).reshape(1, 8, 9, CAP)
    sides = jnp.arange(2).reshape(2, 1, 1, 1) == core
    pieces = jnp.where(sides, pieces, jnp.zeros_like(pieces)).reshape(16, 9, CAP)
    piece = jnp.sum(lax.all_to_all(pieces, ("s", "z", "c"), 0, 0).astype(jnp.float32), axis=0)
    return (grad_input.reshape(frame_input.shape), piece.T)


def solution(mesh):
    fine = Mesh(mesh.devices.reshape(SHAPE), ALL)
    return jax.shard_map(
        local,
        mesh=fine,
        in_specs=(
            P("s", None, SEQ, None),
            P("s", None, SEQ, None),
            P("s", None, SEQ, None),
            P("s", None, SEQ, None),
            P(SEQ, None),
            P(SEQ, None),
            P(ALL, None, None),
            P(None, "s", None),
            P(),
            P(),
            P(),
        ),
        out_specs=(P(ALL, None, None), P(None, ALL)),
        check_vma=False,
    )
```

```python
import math

import jax
import jax.numpy as jnp
import numpy as np
from jax import lax
from jax.experimental import pallas as pl
from jax.experimental.pallas import tpu as pltpu
from jax.sharding import Mesh, PartitionSpec as P

HEADS = 16
HEAD_DIM = 72


CONTRACT_LAST = (((1,), (1,)), ((), ()))


CONTRACT_FIRST = (((0,), (0,)), ((), ()))
SCALE = 1.0 / math.sqrt(HEAD_DIM)
CAP = 300
CAP_PAD = 384


def dot(a, b, dims=(((1,), (0,)), ((), ()))):
    return lax.dot_general(a, b, dims, preferred_element_type=jnp.float32)


def softmax(scores):
    weights = jnp.exp(scores - jnp.max(scores, axis=-1, keepdims=True))
    return weights / jnp.sum(weights, axis=-1, keepdims=True)


def score_grads(attention, prob_grad):
    centred = prob_grad - jnp.sum(prob_grad * attention, axis=-1, keepdims=True)
    return (attention * centred * SCALE).astype(jnp.bfloat16)


def temporal_kernel(grad_ref, query_ref, key_ref, value_ref, out_ref):
    rows, width = grad_ref.shape
    frames = rows // 2
    same = (lax.broadcasted_iota(jnp.int32, (rows, rows), 0) < frames) == (
        lax.broadcasted_iota(jnp.int32, (rows, rows), 1) < frames
    )
    for head in range(HEADS):
        at = slice(head * HEAD_DIM, (head + 1) * HEAD_DIM)
        grad, query, key_rows, value = (
            ref[:, at] for ref in (grad_ref, query_ref, key_ref, value_ref)
        )
        scores = jnp.where(same, dot(query, key_rows, CONTRACT_LAST) * SCALE, -jnp.inf)
        attention = softmax(scores)
        score_grad = score_grads(attention, dot(grad, value, CONTRACT_LAST))
        for part, result in enumerate(
            (
                dot(score_grad, key_rows),
                dot(score_grad, query, CONTRACT_FIRST),
                dot(attention.astype(jnp.bfloat16), grad, CONTRACT_FIRST),
            )
        ):
            start = part * width + head * HEAD_DIM
            out_ref[:, start : start + HEAD_DIM] = result.astype(jnp.bfloat16)


def temporal_grads(grad_heads, query, key_rows, value):
    rows, width = grad_heads.shape
    return pl.pallas_call(
        temporal_kernel,
        out_shape=jax.ShapeDtypeStruct((rows, 3 * width), jnp.bfloat16),
        compiler_params=pltpu.CompilerParams(vmem_limit_bytes=24 << 20),
        cost_estimate=pl.CostEstimate(
            flops=rows * width, bytes_accessed=2 * rows * width, transcendentals=0
        ),
        name="temporal_grads",
    )(grad_heads, query, key_rows, value)


def mixed_kernel(
    place_ref, mine_ref, other_ref, residual_ref, w0, w1, w2, w3, out_ref, held, rows_ref, added, sems
):
    copies = [
        pltpu.make_async_copy(block, held.at[place_ref[i]], sems.at[i])
        for i, block in enumerate((w0, w1, w2, w3))
    ]
    copies.append(pltpu.make_async_copy(residual_ref, added, sems.at[4]))
    for copy in copies:
        copy.start()
    rows_ref[place_ref[4]] = mine_ref[...]
    rows_ref[1 - place_ref[4]] = other_ref[...]
    for copy in copies:
        copy.wait()
    depth = held.shape[2]
    product = dot(
        rows_ref[...].reshape(-1, depth), held[...].reshape(-1, depth), CONTRACT_LAST
    )
    made = product.shape[1]
    out_ref[:, :made] = (added[:, :made].astype(jnp.float32) + product).astype(jnp.bfloat16)
    out_ref[:, made:] = jnp.zeros((out_ref.shape[0], out_ref.shape[1] - made), jnp.bfloat16)


def mixed_half(places, mine, other, residual, blocks):
    in_vmem = pl.BlockSpec(memory_space=pltpu.VMEM)
    rows, depth = mine.shape
    return pl.pallas_call(
        mixed_kernel,
        in_specs=[pl.BlockSpec(memory_space=pltpu.SMEM), in_vmem, in_vmem]
        + [pl.BlockSpec(memory_space=pl.ANY)] * 5,
        out_specs=in_vmem,
        out_shape=jax.ShapeDtypeStruct(residual.shape, jnp.bfloat16),
        scratch_shapes=[
            pltpu.VMEM((4,) + blocks[0].shape, jnp.bfloat16),
            pltpu.VMEM((2, rows, depth), jnp.bfloat16),
            pltpu.VMEM(residual.shape, jnp.bfloat16),
            pltpu.SemaphoreType.DMA((5,)),
        ],
        compiler_params=pltpu.CompilerParams(vmem_limit_bytes=24 << 20),
        cost_estimate=pl.CostEstimate(
            flops=2 * residual.size * depth, bytes_accessed=8 << 20, transcendentals=0
        ),
        name="mixed_half",
    )(places, mine, other, residual, *blocks)


def probs_kernel(length_ref, query_ref, key_ref, probs_ref):
    rows = query_ref.shape[0]
    valid = lax.broadcasted_iota(jnp.int32, (rows, CAP_PAD), 1) < length_ref[0]
    for head in range(HEADS):
        at = slice(head * HEAD_DIM, (head + 1) * HEAD_DIM)
        scores = dot(query_ref[:, at], key_ref[:, at], CONTRACT_LAST) * SCALE
        probs_ref[head] = softmax(jnp.where(valid, scores, -1e30))


def cross_probs(cap_length, cross_query, cap_key):
    rows, width = cross_query.shape
    in_vmem = pl.BlockSpec(memory_space=pltpu.VMEM)
    return pl.pallas_call(
        probs_kernel,
        in_specs=[pl.BlockSpec(memory_space=pltpu.SMEM), in_vmem, in_vmem],
        out_specs=in_vmem,
        out_shape=jax.ShapeDtypeStruct((HEADS, rows, CAP_PAD), jnp.float32),
        compiler_params=pltpu.CompilerParams(vmem_limit_bytes=16 << 20),
        cost_estimate=pl.CostEstimate(
            flops=2 * rows * CAP_PAD * width,
            bytes_accessed=4 << 20,
            transcendentals=HEADS * rows * CAP_PAD,
        ),
        name="cross_probs",
    )(cap_length, cross_query, cap_key)


def cross_kernel(
    core_ref,
    arrived_hbm,
    w_out_hbm,
    query_hbm,
    value_hbm,
    probs_hbm,
    key_hbm,
    cq_ref,
    keep_ref,
    send_ref,
    arrived_ref,
    w_out_ref,
    query_ref,
    value_ref,
    probs_ref,
    key_ref,
    og_ref,
    sems,
):
    held = (arrived_ref, w_out_ref, query_ref, value_ref, probs_ref, key_ref)
    given = (arrived_hbm, w_out_hbm, query_hbm, value_hbm, probs_hbm, key_hbm)
    copies = [
        pltpu.make_async_copy(source, target, sems.at[i])
        for i, (source, target) in enumerate(zip(given, held))
    ]
    for copy in copies:
        copy.start()
    for copy in copies[:2]:
        copy.wait()
    og_ref[...] = dot(arrived_ref[...], w_out_ref[...]).astype(jnp.bfloat16)
    for copy in copies[2:]:
        copy.wait()
    first = core_ref[0] == 0
    for head in range(HEADS):
        at = slice(head * HEAD_DIM, (head + 1) * HEAD_DIM)
        query, out_grad, key_rows, value = (
            ref[:, at] for ref in (query_ref, og_ref, key_ref, value_ref)
        )
        attention = probs_ref[head]
        score_grad = score_grads(attention, dot(out_grad, value, CONTRACT_LAST))
        cq_ref[:, at] = dot(score_grad, key_rows).astype(jnp.bfloat16)
        key_term = dot(query, score_grad, CONTRACT_FIRST)
        value_term = dot(out_grad, attention.astype(jnp.bfloat16), CONTRACT_FIRST)
        keep_ref[head] = jnp.where(first, key_term, value_term).astype(jnp.bfloat16)
        send_ref[head] = jnp.where(first, value_term, key_term).astype(jnp.bfloat16)


def cross_grads(core, arrived, w_out, cross_query, cap_value, probs, cap_key):
    rows, width = cross_query.shape
    in_vmem = pl.BlockSpec(memory_space=pltpu.VMEM)
    copied = (arrived, w_out, cross_query, cap_value, probs, cap_key)
    term = jax.ShapeDtypeStruct((HEADS, HEAD_DIM, CAP_PAD), jnp.bfloat16)
    return pl.pallas_call(
        cross_kernel,
        in_specs=[pl.BlockSpec(memory_space=pltpu.SMEM)]
        + [pl.BlockSpec(memory_space=pl.ANY)] * 6,
        out_specs=(in_vmem,) * 3,
        out_shape=(jax.ShapeDtypeStruct((rows, width), jnp.bfloat16), term, term),
        scratch_shapes=[pltpu.VMEM(array.shape, array.dtype) for array in copied]
        + [pltpu.VMEM((rows, width), jnp.bfloat16), pltpu.SemaphoreType.DMA((6,))],
        compiler_params=pltpu.CompilerParams(vmem_limit_bytes=56 << 20),
        cost_estimate=pl.CostEstimate(
            flops=8 * rows * CAP_PAD * width + 2 * rows * width * arrived.shape[1],
            bytes_accessed=12 << 20,
            transcendentals=0,
        ),
        name="cross_grads",
    )(core, *copied)


ALL = ("s", "x", "y", "z", "c")
SEQ = ("x", "y", "z", "c")
SHAPE = (2, 4, 4, 4, 2)


def flat(s, x, y, z, c):
    return (((s * 4 + x) * 4 + y) * 4 + z) * 2 + c


def ring_groups(first):
    groups = []
    for s in range(2):
        for z in range(4):
            for fixed in range(4):
                groups.append([flat(s, i, fixed, z, first) for i in range(4)])
                groups.append([flat(s, fixed, i, z, 1 - first) for i in range(4)])
    return groups


def gather_groups(block, groups):
    copies = jnp.broadcast_to(block[None], (4,) + block.shape)
    return lax.all_to_all(copies, ALL, 0, 0, axis_index_groups=groups)


def shift_last(block, step):
    pairs = []
    for s in range(2):
        for x in range(4):
            for y in range(4):
                for z in range(4):
                    pairs.append((flat(s, x, y, z, 0), flat(s, x, (y + step) % 4, z, 0)))
                    pairs.append((flat(s, x, y, z, 1), flat(s, (x + step) % 4, y, z, 1)))
    return lax.ppermute(block, ALL, pairs)


def swap_cores(block):
    return lax.ppermute(block, "c", [(0, 1), (1, 0)])


def in_core_order(mine, other):
    core = lax.axis_index("c")
    return jnp.stack([jnp.where(core == 0, mine, other), jnp.where(core == 0, other, mine)])


def feature_order():
    order = np.full((2, 640), -1, np.int32)
    for c in range(2):
        for i in range(4):
            for j in range(4):
                x, y = (j, i) if c == 0 else (i, j)
                for q in range(36):
                    at = (4 * i + j) * 36 + q
                    order[c, at] = 72 * (4 * x + y) + 18 * (q // 9) + 9 * c + q % 9
    return order.reshape(1280)


def cross_fetch(part):
    def place(z):
        return (z % 2, z // 2)

    pairs = []
    for x in range(4):
        for y in range(4):
            for z in range(8):
                for c in range(2):
                    to = (z + (1 if c == 0 else 7)) % 8
                    s0, z0 = place(z)
                    s1, z1 = place(to)
                    pairs.append((flat(s0, x, y, z0, c), flat(s1, x, y, z1, c)))
    return lax.ppermute(part, ALL, pairs)


def cross_whole(cross_weights, got):
    core = lax.axis_index("c")
    side = lax.axis_index("s")
    swapped = lax.ppermute(got, "c", [(0, 1), (1, 0)])
    other = jnp.stack([jnp.where(core == 0, got, swapped), jnp.where(core == 0, swapped, got)])
    low = jnp.where(side == 0, cross_weights, other)
    high = jnp.where(side == 0, other, cross_weights)
    return jnp.concatenate([low, high], axis=1)


def local(
    grad_out,
    t_query,
    t_key,
    t_value,
    t_out_weight,
    t_qkv_weight,
    frame_input,
    cross_weights,
    cap_key,
    cap_value,
    cap_length,
):
    width = grad_out.shape[-1]
    core = lax.axis_index("c")
    grad_rows = grad_out.reshape(-1, width)
    rows = grad_rows.shape[0]
    place = (jnp.asarray(feature_order())[:, None] == jnp.arange(width)[None, :]).astype(
        jnp.bfloat16
    )
    place_mine = lax.dynamic_slice(place, (core * 640, 0), (640, width))
    grad_both = in_core_order(grad_rows, swap_cores(grad_rows)).reshape(2 * rows, width)
    shard = jnp.concatenate([t_out_weight, t_qkv_weight], axis=1).reshape(2, -1)
    column = lax.all_to_all(jnp.broadcast_to(shard[None], (4,) + shard.shape), "z", 0, 0)
    column = jnp.pad(column.reshape(36, 4 * width), ((0, 4), (0, 0)))
    near = gather_groups(column, ring_groups(0))
    residual = lax.dot_general(
        grad_both, place_mine, CONTRACT_LAST, preferred_element_type=jnp.float32
    ).astype(jnp.bfloat16)
    padding = ((0, CAP_PAD - CAP), (0, 0))
    cap_key, cap_value = jnp.pad(cap_key, padding), jnp.pad(cap_value, padding)
    out_near = near[:, :36, :width].reshape(144, width)
    cross_part = lax.dynamic_index_in_dim(cross_weights, core, 0, keepdims=False)
    out_near, cross_part, grad_both, residual, place, cap_key, cap_value = (
        lax.optimization_barrier(
            (out_near, cross_part, grad_both, residual, place, cap_key, cap_value)
        )
    )
    qkv_near = near[:, :36, width:].reshape(144, 3 * width)
    blocks = [qkv_near] + [shift_last(qkv_near, step) for step in (1, 3, 2)]
    place_here = jnp.where(core == 0, lax.axis_index("y"), lax.axis_index("x"))
    slots = (place_here - jnp.array([0, 1, 3, 2], jnp.int32)) % 4
    places = jnp.concatenate([slots, core.reshape(1)])
    out_mine = gather_groups(out_near, ring_groups(1)).reshape(576, width)
    cross_part = cross_fetch(cross_part)
    heads_mine = (
        lax.dot_general(grad_both, out_mine, CONTRACT_LAST, preferred_element_type=jnp.float32)
        .astype(jnp.bfloat16)
        .reshape(2, rows, 576)
    )
    kept = lax.dynamic_index_in_dim(heads_mine, core, 0, keepdims=False)
    sent = lax.dynamic_index_in_dim(heads_mine, 1 - core, 0, keepdims=False)
    heads_parts = in_core_order(kept, swap_cores(sent))
    grad_heads = (
        jnp.dot(heads_parts[0], place[:576], preferred_element_type=jnp.float32)
        + jnp.dot(heads_parts[1], place[640:1216], preferred_element_type=jnp.float32)
    ).astype(jnp.bfloat16)
    qkv_grad = temporal_grads(
        grad_heads, *(saved.reshape(rows, width) for saved in (t_query, t_key, t_value))
    )
    qkv_grad, cross_part, *blocks = lax.optimization_barrier((qkv_grad, cross_part, *blocks))
    full_cross = cross_whole(cross_weights, cross_part)
    mixed = mixed_half(
        places, qkv_grad, swap_cores(qkv_grad), residual, blocks
    ).reshape(2, rows, 640)
    w_out_placed = lax.dot_general(
        place, full_cross[1], CONTRACT_LAST, preferred_element_type=jnp.float32
    ).astype(jnp.bfloat16)
    cross_query = jnp.dot(
        frame_input.reshape(rows, width), full_cross[0], preferred_element_type=jnp.float32
    ).astype(jnp.bfloat16)
    probs = cross_probs(cap_length, cross_query, cap_key)
    arrived = lax.all_to_all(mixed.transpose(1, 0, 2), SEQ, split_axis=0, concat_axis=0)
    arrived = arrived.reshape(64, 2, 2, 640).transpose(0, 2, 1, 3).reshape(128, 1280)
    cq_grad, keep, send = cross_grads(
        core.reshape(1), arrived, w_out_placed, cross_query, cap_value, probs, cap_key
    )
    chip = (keep.astype(jnp.float32) + swap_cores(send).astype(jnp.float32)).astype(jnp.bfloat16)
    grad_input = (
        jnp.dot(arrived, place, preferred_element_type=jnp.float32)
        + lax.dot_general(cq_grad, full_cross[0], CONTRACT_LAST, preferred_element_type=jnp.float32)
    ).astype(jnp.bfloat16)
    head = jnp.sum(lax.all_to_all(chip, ("x", "y"), 0, 0).astype(jnp.float32), axis=0)
    pieces = head[:, :CAP].astype(jnp.bfloat16).reshape(1, 8, 9, CAP)
    sides = jnp.arange(2).reshape(2, 1, 1, 1) == core
    pieces = jnp.where(sides, pieces, jnp.zeros_like(pieces)).reshape(16, 9, CAP)
    piece = jnp.sum(lax.all_to_all(pieces, ("s", "z", "c"), 0, 0).astype(jnp.float32), axis=0)
    return (grad_input.reshape(frame_input.shape), piece.T)


def solution(mesh):
    fine = Mesh(mesh.devices.reshape(SHAPE), ALL)
    return jax.shard_map(
        local,
        mesh=fine,
        in_specs=(
            P("s", None, SEQ, None),
            P("s", None, SEQ, None),
            P("s", None, SEQ, None),
            P("s", None, SEQ, None),
            P(SEQ, None),
            P(SEQ, None),
            P(ALL, None, None),
            P(None, "s", None),
            P(),
            P(),
            P(),
        ),
        out_specs=(P(ALL, None, None), P(None, ALL)),
        check_vma=False,
    )
```

```python
import math

import jax
import jax.numpy as jnp
import numpy as np
from jax import lax
from jax.experimental import pallas as pl
from jax.experimental.pallas import tpu as pltpu
from jax.sharding import Mesh, PartitionSpec as P

HEADS = 16
HEAD_DIM = 72


CONTRACT_LAST = (((1,), (1,)), ((), ()))


CONTRACT_FIRST = (((0,), (0,)), ((), ()))
SCALE = 1.0 / math.sqrt(HEAD_DIM)
CAP = 300
CAP_PAD = 384


def dot(a, b, dims=(((1,), (0,)), ((), ()))):
    return lax.dot_general(a, b, dims, preferred_element_type=jnp.float32)


def softmax(scores):
    weights = jnp.exp(scores - jnp.max(scores, axis=-1, keepdims=True))
    return weights / jnp.sum(weights, axis=-1, keepdims=True)


def score_grads(attention, prob_grad):
    centred = prob_grad - jnp.sum(prob_grad * attention, axis=-1, keepdims=True)
    return (attention * centred * SCALE).astype(jnp.bfloat16)


def temporal_kernel(grad_ref, query_ref, key_ref, value_ref, out_ref):
    rows, width = grad_ref.shape
    frames = rows // 2
    same = (lax.broadcasted_iota(jnp.int32, (rows, rows), 0) < frames) == (
        lax.broadcasted_iota(jnp.int32, (rows, rows), 1) < frames
    )
    for head in range(HEADS):
        at = slice(head * HEAD_DIM, (head + 1) * HEAD_DIM)
        grad, query, key_rows, value = (
            ref[:, at] for ref in (grad_ref, query_ref, key_ref, value_ref)
        )
        scores = jnp.where(same, dot(query, key_rows, CONTRACT_LAST) * SCALE, -jnp.inf)
        attention = softmax(scores)
        score_grad = score_grads(attention, dot(grad, value, CONTRACT_LAST))
        for part, result in enumerate(
            (
                dot(score_grad, key_rows),
                dot(score_grad, query, CONTRACT_FIRST),
                dot(attention.astype(jnp.bfloat16), grad, CONTRACT_FIRST),
            )
        ):
            start = part * width + head * HEAD_DIM
            out_ref[:, start : start + HEAD_DIM] = result.astype(jnp.bfloat16)


def temporal_grads(grad_heads, query, key_rows, value):
    rows, width = grad_heads.shape
    return pl.pallas_call(
        temporal_kernel,
        out_shape=jax.ShapeDtypeStruct((rows, 3 * width), jnp.bfloat16),
        compiler_params=pltpu.CompilerParams(vmem_limit_bytes=24 << 20),
        cost_estimate=pl.CostEstimate(
            flops=rows * width, bytes_accessed=2 * rows * width, transcendentals=0
        ),
        name="temporal_grads",
    )(grad_heads, query, key_rows, value)


def mixed_kernel(
    place_ref, mine_ref, other_ref, residual_ref, w0, w1, w2, w3, out_ref, held, rows_ref, added, sems
):
    copies = [
        pltpu.make_async_copy(block, held.at[place_ref[i]], sems.at[i])
        for i, block in enumerate((w0, w1, w2, w3))
    ]
    copies.append(pltpu.make_async_copy(residual_ref, added, sems.at[4]))
    for copy in copies:
        copy.start()
    rows_ref[place_ref[4]] = mine_ref[...]
    rows_ref[1 - place_ref[4]] = other_ref[...]
    for copy in copies:
        copy.wait()
    depth = held.shape[2]
    product = dot(
        rows_ref[...].reshape(-1, depth), held[...].reshape(-1, depth), CONTRACT_LAST
    )
    made = product.shape[1]
    out_ref[:, :made] = (added[:, :made].astype(jnp.float32) + product).astype(jnp.bfloat16)
    out_ref[:, made:] = jnp.zeros((out_ref.shape[0], out_ref.shape[1] - made), jnp.bfloat16)


def mixed_half(places, mine, other, residual, blocks):
    in_vmem = pl.BlockSpec(memory_space=pltpu.VMEM)
    rows, depth = mine.shape
    return pl.pallas_call(
        mixed_kernel,
        in_specs=[pl.BlockSpec(memory_space=pltpu.SMEM), in_vmem, in_vmem]
        + [pl.BlockSpec(memory_space=pl.ANY)] * 5,
        out_specs=in_vmem,
        out_shape=jax.ShapeDtypeStruct(residual.shape, jnp.bfloat16),
        scratch_shapes=[
            pltpu.VMEM((4,) + blocks[0].shape, jnp.bfloat16),
            pltpu.VMEM((2, rows, depth), jnp.bfloat16),
            pltpu.VMEM(residual.shape, jnp.bfloat16),
            pltpu.SemaphoreType.DMA((5,)),
        ],
        compiler_params=pltpu.CompilerParams(vmem_limit_bytes=24 << 20),
        cost_estimate=pl.CostEstimate(
            flops=2 * residual.size * depth, bytes_accessed=8 << 20, transcendentals=0
        ),
        name="mixed_half",
    )(places, mine, other, residual, *blocks)


def probs_kernel(length_ref, query_ref, key_ref, probs_ref):
    rows = query_ref.shape[0]
    valid = lax.broadcasted_iota(jnp.int32, (rows, CAP_PAD), 1) < length_ref[0]
    for head in range(HEADS):
        at = slice(head * HEAD_DIM, (head + 1) * HEAD_DIM)
        scores = dot(query_ref[:, at], key_ref[:, at], CONTRACT_LAST) * SCALE
        probs_ref[head] = softmax(jnp.where(valid, scores, -1e30))


def cross_probs(cap_length, cross_query, cap_key):
    rows, width = cross_query.shape
    in_vmem = pl.BlockSpec(memory_space=pltpu.VMEM)
    return pl.pallas_call(
        probs_kernel,
        in_specs=[pl.BlockSpec(memory_space=pltpu.SMEM), in_vmem, in_vmem],
        out_specs=in_vmem,
        out_shape=jax.ShapeDtypeStruct((HEADS, rows, CAP_PAD), jnp.float32),
        compiler_params=pltpu.CompilerParams(vmem_limit_bytes=16 << 20),
        cost_estimate=pl.CostEstimate(
            flops=2 * rows * CAP_PAD * width,
            bytes_accessed=4 << 20,
            transcendentals=HEADS * rows * CAP_PAD,
        ),
        name="cross_probs",
    )(cap_length, cross_query, cap_key)


def cross_kernel(
    core_ref,
    arrived_hbm,
    w_out_hbm,
    query_hbm,
    value_hbm,
    probs_hbm,
    key_hbm,
    cq_ref,
    keep_ref,
    send_ref,
    arrived_ref,
    w_out_ref,
    query_ref,
    value_ref,
    probs_ref,
    key_ref,
    og_ref,
    sems,
):
    held = (arrived_ref, w_out_ref, query_ref, value_ref, probs_ref, key_ref)
    given = (arrived_hbm, w_out_hbm, query_hbm, value_hbm, probs_hbm, key_hbm)
    copies = [
        pltpu.make_async_copy(source, target, sems.at[i])
        for i, (source, target) in enumerate(zip(given, held))
    ]
    for copy in copies:
        copy.start()
    for copy in copies[:2]:
        copy.wait()
    og_ref[...] = dot(arrived_ref[...], w_out_ref[...]).astype(jnp.bfloat16)
    for copy in copies[2:]:
        copy.wait()
    first = core_ref[0] == 0
    for head in range(HEADS):
        at = slice(head * HEAD_DIM, (head + 1) * HEAD_DIM)
        query, out_grad, key_rows, value = (
            ref[:, at] for ref in (query_ref, og_ref, key_ref, value_ref)
        )
        attention = probs_ref[head]
        score_grad = score_grads(attention, dot(out_grad, value, CONTRACT_LAST))
        cq_ref[:, at] = dot(score_grad, key_rows).astype(jnp.bfloat16)
        key_term = dot(query, score_grad, CONTRACT_FIRST)
        value_term = dot(out_grad, attention.astype(jnp.bfloat16), CONTRACT_FIRST)
        keep_ref[head] = jnp.where(first, key_term, value_term).astype(jnp.bfloat16)
        send_ref[head] = jnp.where(first, value_term, key_term).astype(jnp.bfloat16)


def cross_grads(core, arrived, w_out, cross_query, cap_value, probs, cap_key):
    rows, width = cross_query.shape
    in_vmem = pl.BlockSpec(memory_space=pltpu.VMEM)
    copied = (arrived, w_out, cross_query, cap_value, probs, cap_key)
    term = jax.ShapeDtypeStruct((HEADS, HEAD_DIM, CAP_PAD), jnp.bfloat16)
    return pl.pallas_call(
        cross_kernel,
        in_specs=[pl.BlockSpec(memory_space=pltpu.SMEM)]
        + [pl.BlockSpec(memory_space=pl.ANY)] * 6,
        out_specs=(in_vmem,) * 3,
        out_shape=(jax.ShapeDtypeStruct((rows, width), jnp.bfloat16), term, term),
        scratch_shapes=[pltpu.VMEM(array.shape, array.dtype) for array in copied]
        + [pltpu.VMEM((rows, width), jnp.bfloat16), pltpu.SemaphoreType.DMA((6,))],
        compiler_params=pltpu.CompilerParams(vmem_limit_bytes=50 << 20),
        cost_estimate=pl.CostEstimate(
            flops=8 * rows * CAP_PAD * width + 2 * rows * width * arrived.shape[1],
            bytes_accessed=12 << 20,
            transcendentals=0,
        ),
        name="cross_grads",
    )(core, *copied)


ALL = ("s", "x", "y", "z", "c")
SEQ = ("x", "y", "z", "c")
SHAPE = (2, 4, 4, 4, 2)


def flat(s, x, y, z, c):
    return (((s * 4 + x) * 4 + y) * 4 + z) * 2 + c


def ring_groups(first):
    groups = []
    for s in range(2):
        for z in range(4):
            for fixed in range(4):
                groups.append([flat(s, i, fixed, z, first) for i in range(4)])
                groups.append([flat(s, fixed, i, z, 1 - first) for i in range(4)])
    return groups


def gather_groups(block, groups):
    copies = jnp.broadcast_to(block[None], (4,) + block.shape)
    return lax.all_to_all(copies, ALL, 0, 0, axis_index_groups=groups)


def shift_last(block, step):
    pairs = []
    for s in range(2):
        for x in range(4):
            for y in range(4):
                for z in range(4):
                    pairs.append((flat(s, x, y, z, 0), flat(s, x, (y + step) % 4, z, 0)))
                    pairs.append((flat(s, x, y, z, 1), flat(s, (x + step) % 4, y, z, 1)))
    return lax.ppermute(block, ALL, pairs)


def swap_cores(block):
    return lax.ppermute(block, "c", [(0, 1), (1, 0)])


def in_core_order(mine, other):
    core = lax.axis_index("c")
    return jnp.stack([jnp.where(core == 0, mine, other), jnp.where(core == 0, other, mine)])


def feature_order():
    order = np.full((2, 640), -1, np.int32)
    for c in range(2):
        for i in range(4):
            for j in range(4):
                x, y = (j, i) if c == 0 else (i, j)
                for q in range(36):
                    at = (4 * i + j) * 36 + q
                    order[c, at] = 72 * (4 * x + y) + 18 * (q // 9) + 9 * c + q % 9
    return order.reshape(1280)


def cross_fetch(part):
    def place(z):
        return (z % 2, z // 2)

    pairs = []
    for x in range(4):
        for y in range(4):
            for z in range(8):
                for c in range(2):
                    to = (z + (1 if c == 0 else 7)) % 8
                    s0, z0 = place(z)
                    s1, z1 = place(to)
                    pairs.append((flat(s0, x, y, z0, c), flat(s1, x, y, z1, c)))
    return lax.ppermute(part, ALL, pairs)


def cross_whole(cross_weights, got):
    core = lax.axis_index("c")
    side = lax.axis_index("s")
    swapped = lax.ppermute(got, "c", [(0, 1), (1, 0)])
    other = jnp.stack([jnp.where(core == 0, got, swapped), jnp.where(core == 0, swapped, got)])
    low = jnp.where(side == 0, cross_weights, other)
    high = jnp.where(side == 0, other, cross_weights)
    return jnp.concatenate([low, high], axis=1)


def local(
    grad_out,
    t_query,
    t_key,
    t_value,
    t_out_weight,
    t_qkv_weight,
    frame_input,
    cross_weights,
    cap_key,
    cap_value,
    cap_length,
):
    width = grad_out.shape[-1]
    core = lax.axis_index("c")
    grad_rows = grad_out.reshape(-1, width)
    rows = grad_rows.shape[0]
    place = (jnp.asarray(feature_order())[:, None] == jnp.arange(width)[None, :]).astype(
        jnp.bfloat16
    )
    place_mine = lax.dynamic_slice(place, (core * 640, 0), (640, width))
    grad_both = in_core_order(grad_rows, swap_cores(grad_rows)).reshape(2 * rows, width)
    shard = jnp.concatenate([t_out_weight, t_qkv_weight], axis=1).reshape(2, -1)
    column = lax.all_to_all(jnp.broadcast_to(shard[None], (4,) + shard.shape), "z", 0, 0)
    column = jnp.pad(column.reshape(36, 4 * width), ((0, 4), (0, 0)))
    near = gather_groups(column, ring_groups(0))
    residual = lax.dot_general(
        grad_both, place_mine, CONTRACT_LAST, preferred_element_type=jnp.float32
    ).astype(jnp.bfloat16)
    padding = ((0, CAP_PAD - CAP), (0, 0))
    cap_key, cap_value = jnp.pad(cap_key, padding), jnp.pad(cap_value, padding)
    out_near = near[:, :36, :width].reshape(144, width)
    cross_part = lax.dynamic_index_in_dim(cross_weights, core, 0, keepdims=False)
    out_near, cross_part, grad_both, residual, place, cap_key, cap_value = (
        lax.optimization_barrier(
            (out_near, cross_part, grad_both, residual, place, cap_key, cap_value)
        )
    )
    qkv_near = near[:, :36, width:].reshape(144, 3 * width)
    blocks = [qkv_near] + [shift_last(qkv_near, step) for step in (1, 3, 2)]
    place_here = jnp.where(core == 0, lax.axis_index("y"), lax.axis_index("x"))
    slots = (place_here - jnp.array([0, 1, 3, 2], jnp.int32)) % 4
    places = jnp.concatenate([slots, core.reshape(1)])
    out_mine = gather_groups(out_near, ring_groups(1)).reshape(576, width)
    cross_part = cross_fetch(cross_part)
    heads_mine = (
        lax.dot_general(grad_both, out_mine, CONTRACT_LAST, preferred_element_type=jnp.float32)
        .astype(jnp.bfloat16)
        .reshape(2, rows, 576)
    )
    kept = lax.dynamic_index_in_dim(heads_mine, core, 0, keepdims=False)
    sent = lax.dynamic_index_in_dim(heads_mine, 1 - core, 0, keepdims=False)
    heads_parts = in_core_order(kept, swap_cores(sent))
    grad_heads = (
        jnp.dot(heads_parts[0], place[:576], preferred_element_type=jnp.float32)
        + jnp.dot(heads_parts[1], place[640:1216], preferred_element_type=jnp.float32)
    ).astype(jnp.bfloat16)
    qkv_grad = temporal_grads(
        grad_heads, *(saved.reshape(rows, width) for saved in (t_query, t_key, t_value))
    )
    qkv_grad, cross_part, *blocks = lax.optimization_barrier((qkv_grad, cross_part, *blocks))
    full_cross = cross_whole(cross_weights, cross_part)
    mixed = mixed_half(
        places, qkv_grad, swap_cores(qkv_grad), residual, blocks
    ).reshape(2, rows, 640)
    w_out_placed = lax.dot_general(
        place, full_cross[1], CONTRACT_LAST, preferred_element_type=jnp.float32
    ).astype(jnp.bfloat16)
    cross_query = jnp.dot(
        frame_input.reshape(rows, width), full_cross[0], preferred_element_type=jnp.float32
    ).astype(jnp.bfloat16)
    probs = cross_probs(cap_length, cross_query, cap_key)
    arrived = lax.all_to_all(mixed.transpose(1, 0, 2), SEQ, split_axis=0, concat_axis=0)
    arrived = arrived.reshape(64, 2, 2, 640).transpose(0, 2, 1, 3).reshape(128, 1280)
    cq_grad, keep, send = cross_grads(
        core.reshape(1), arrived, w_out_placed, cross_query, cap_value, probs, cap_key
    )
    chip = (keep.astype(jnp.float32) + swap_cores(send).astype(jnp.float32)).astype(jnp.bfloat16)
    grad_input = (
        jnp.dot(arrived, place, preferred_element_type=jnp.float32)
        + lax.dot_general(cq_grad, full_cross[0], CONTRACT_LAST, preferred_element_type=jnp.float32)
    ).astype(jnp.bfloat16)
    head = jnp.sum(lax.all_to_all(chip, ("x", "y"), 0, 0).astype(jnp.float32), axis=0)
    pieces = head[:, :CAP].astype(jnp.bfloat16).reshape(1, 8, 9, CAP)
    sides = jnp.arange(2).reshape(2, 1, 1, 1) == core
    pieces = jnp.where(sides, pieces, jnp.zeros_like(pieces)).reshape(16, 9, CAP)
    piece = jnp.sum(lax.all_to_all(pieces, ("s", "z", "c"), 0, 0).astype(jnp.float32), axis=0)
    return (grad_input.reshape(frame_input.shape), piece.T)


def solution(mesh):
    fine = Mesh(mesh.devices.reshape(SHAPE), ALL)
    return jax.shard_map(
        local,
        mesh=fine,
        in_specs=(
            P("s", None, SEQ, None),
            P("s", None, SEQ, None),
            P("s", None, SEQ, None),
            P("s", None, SEQ, None),
            P(SEQ, None),
            P(SEQ, None),
            P(ALL, None, None),
            P(None, "s", None),
            P(),
            P(),
            P(),
        ),
        out_specs=(P(ALL, None, None), P(None, ALL)),
        check_vma=False,
    )
```
